512 devices in a mesh: chan: 32 (over y_hi, z), tm: 16 (over y_lo, x, core).
Axes of the slice: x: 4, y: 8 (y_hi: 4, y_lo: 2; y = y_hi * 2 + y_lo), z: 8, core: 2. Of those that a mesh axis runs over, the one named last changes fastest.
Arguments:
- strain_record: bfloat16 [4096, 131072], P('chan', 'tm')
- dead_channels: int32 [200], replicated, may hold values from 1 to 4094, as said below
- source_channels: int32 [1024], P('chan'), may hold values from 0 to 4095, as said below
- band_start: int32 [1], replicated, may hold values from 1 to 176
Outputs:
- cross_spectra: bfloat16 [2, 80, 1024, 4096], P(None, 'tm', None, 'chan')
The draws below stay inside these ranges and needn't reach their ends.
Inputs may be any that keep to these rules, and one draw needn't show every extreme that they name: `dead_channels`: distinct channel indices. `source_channels`: each block of 128 consecutive channels holds exactly 32 sources, in increasing order; entry s lies in block s // 32.
All inputs are finite; a program needn't handle non-finite values.
Results may differ from the reference program's by a relative error of at most 0.0056.
Values may be sent and summed in bfloat16 or wider, within the bound.
A program may use at most 64 MiB of HBM per device.

```python
import jax
import jax.numpy as jnp
from jax import lax

NFFT = 512
SRC_DEV = 32
DEAD = 200
CHANNELS = 4096
BLOCKS = 256
SAMPLES = 131072
NBINS = 80
SOURCES = 1024


def draw_strain_record(key, part):
    key = jax.random.fold_in(key, 11)
    key_noise, key_common, key_scale, key_rough = jax.random.split(key, 4)
    chan_pos = jnp.arange(CHANNELS, dtype=jnp.float32) / CHANNELS
    rough_gain = jax.random.uniform(key_rough, (CHANNELS,), jnp.float32, 0.8, 1.2)
    coupling = (0.5 + chan_pos) * rough_gain
    noise_vals = jax.random.normal(key_noise, (CHANNELS, SAMPLES), jnp.float32)
    chan_scale = jnp.exp(jax.random.uniform(key_scale, (CHANNELS,), jnp.float32, 0.0, 1.4))
    common_vals = 3.0 * jax.random.normal(key_common, (SAMPLES,), jnp.float32)
    values = chan_scale[:, None] * noise_vals + coupling[:, None] * common_vals[None, :]
    return values.astype(jnp.bfloat16)


def draw_dead_channels(key, part):
    key = jax.random.fold_in(key, 12)
    inner = jax.random.permutation(key, CHANNELS - 4)[:DEAD - 2].astype(jnp.int32) + 2
    ends = jnp.array([1, CHANNELS - 2], dtype=jnp.int32)
    return jnp.concatenate([ends, inner]).astype(jnp.int32)


def draw_source_channels(key, part):
    key = jax.random.fold_in(key, 13)
    nblocks = SOURCES // SRC_DEV
    chan_dev = CHANNELS // nblocks
    scores = jax.random.randint(key, (nblocks, chan_dev), 0, 1 << 20, dtype=jnp.int32) * chan_dev
    scores = scores + jnp.arange(chan_dev, dtype=jnp.int32)[None, :]
    forced = 1 << 30
    scores = scores.at[0, 0].set(forced)
    scores = scores.at[nblocks - 1, chan_dev - 1].set(forced)
    chosen = jax.lax.top_k(scores, SRC_DEV)[1].astype(jnp.int32)
    chosen = jnp.sort(chosen, axis=1)
    offsets = jnp.arange(nblocks, dtype=jnp.int32)[:, None] * chan_dev
    return (chosen + offsets).reshape(SOURCES).astype(jnp.int32)


def setup_inputs(seed: int = 0) -> dict:
    key_of = jax.random.split(jax.random.key(seed), 5)
    strain_record = draw_strain_record(jax.random.fold_in(key_of[4], 71), 0)
    dead_channels = draw_dead_channels(jax.random.fold_in(key_of[4], 71), 0)
    source_channels = draw_source_channels(jax.random.fold_in(key_of[4], 71), 0)
    band_start = jax.random.randint(key_of[3], (1,), 1, NFFT // 2 - NBINS + 1).astype(jnp.int32)
    return dict(strain_record=strain_record, dead_channels=dead_channels, source_channels=source_channels, band_start=band_start)


EPS = 1e-06

def make_table(band_start, nbins):
    n_int = jnp.arange(NFFT, dtype=jnp.int32)
    k_int = band_start[0].astype(jnp.int32) + jnp.arange(nbins, dtype=jnp.int32)
    phase_idx = k_int[:, None] * n_int[None, :] % NFFT
    angle_val = 2.0 * jnp.pi / NFFT * phase_idx.astype(jnp.float32)
    taper_val = 0.5 - 0.5 * jnp.cos(2.0 * jnp.pi / NFFT * n_int.astype(jnp.float32))
    cos_part = taper_val[None, :] * jnp.cos(angle_val)
    sin_part = -taper_val[None, :] * jnp.sin(angle_val)
    return jnp.concatenate([cos_part, sin_part], axis=0).astype(jnp.bfloat16)

def reference(strain_record, dead_channels, source_channels, band_start):
    dft_table = make_table(band_start, NBINS)
    chan_ids = jnp.arange(CHANNELS, dtype=jnp.int32)
    live_mask = 1.0 - jnp.any(chan_ids[:, None] == dead_channels[None, :], axis=1).astype(jnp.float32)
    raw_spec = jnp.dot(strain_record.reshape(CHANNELS * BLOCKS, NFFT), dft_table.T, preferred_element_type=jnp.float32).reshape(CHANNELS, BLOCKS * 2 * NBINS)
    common_mode = jnp.dot(live_mask, raw_spec, precision=lax.Precision.HIGHEST) / (CHANNELS - DEAD)
    spectra = (live_mask[:, None] * (raw_spec - common_mode[None, :])).astype(jnp.bfloat16)
    spec_full = spectra.astype(jnp.float32).reshape(CHANNELS, BLOCKS, 2, NBINS)
    power = lax.optimization_barrier(jnp.sum(spec_full * spec_full, axis=(1, 2))) / BLOCKS
    whitened = (spec_full * lax.rsqrt(power + EPS)[:, None, None, :]).astype(jnp.bfloat16)
    source_spec = whitened[source_channels]

    def one_bin(pair):
        src_bin, white_bin = pair

        def mult(left, right):
            return jnp.dot(left, right.T, preferred_element_type=jnp.float32)
        real_part = mult(src_bin[:, :, 0], white_bin[:, :, 0]) + mult(src_bin[:, :, 1], white_bin[:, :, 1])
        imag_part = mult(src_bin[:, :, 0], white_bin[:, :, 1]) - mult(src_bin[:, :, 1], white_bin[:, :, 0])
        return (jnp.stack([real_part, imag_part]) / BLOCKS).astype(jnp.bfloat16)
    per_bin = lax.map(one_bin, (jnp.moveaxis(source_spec, 3, 0), jnp.moveaxis(whitened, 3, 0)))
    return jnp.transpose(per_bin, (1, 0, 2, 3))
```

```python
import jax
import jax.numpy as jnp
import numpy as np
from jax import lax
from jax.experimental import pallas as pl
from jax.experimental.pallas import tpu as pltpu
from jax.sharding import PartitionSpec as P

NFFT = 512
FQ = 5
NT = 16
NY, NZ = 4, 8
CH = 128
SRC = 32
HALF = 16
NCHAN = NY * NZ * CH
BLOCKS = 256
DEAD = 200
ROWS = 2 * FQ * NT
PAD = 256
EPS = 1e-06
NP1, NP2 = 7, 3

UNITS = {(0, 0): (2, 0), (0, 1): (1, 0), (1, 0): (2, 1), (1, 1): (1, 1), (2, 0): (2, 2), (2, 1): (1, 2), (3, 0): (1, 3), (3, 1): (1, 4), (4, 0): (1, 5), (4, 1): (1, 6)}
PLACE = {unit: at for at, unit in UNITS.items()}
EARLY = (0, 1, 2)
GROUPS = ((0, 1), (1, 3), (3, 5))
LATE = 4
TAKE, Y1, Z1, OWN1, Z2, Y2 = range(6)
ORDER = (
    (TAKE, 0, 0), (OWN1, 0, 0), (Y1, 0, 0), (Z2, 0, 0), (TAKE, 1, 0), (OWN1, 1, 0), (Y1, 1, 0), (Z2, 1, 0),
    (OWN1, 2, 0), (Y1, 2, 0), (Z2, 2, 0), (OWN1, 0, 1), (Y1, 0, 1), (Z2, 0, 1), (OWN1, 1, 1), (TAKE, 2, 0),
    (Y1, 3, 0), (Y1, 4, 0), (Y1, 5, 0), (Y1, 6, 0), (Y1, 1, 1), (Z2, 1, 1), (OWN1, 2, 1), (Y1, 2, 1), (Z2, 2, 1),
    (OWN1, 0, 2), (Z1, 0, 0), (Z2, 0, 2), (OWN1, 1, 2), (Z2, 1, 2), (Y1, 3, 1), (OWN1, 2, 2), (Z2, 2, 2),
    (Y1, 4, 1), (OWN1, 0, 3), (Y1, 5, 1), (Z1, 0, 1), (Y1, 6, 1), (Z2, 0, 3), (OWN1, 1, 3), (Z1, 1, 0), (Z1, 2, 0),
    (Z2, 1, 3), (OWN1, 2, 3), (Z1, 3, 0), (Z2, 2, 3), (Z1, 4, 0), (Z1, 5, 0), (Z1, 6, 0), (Z1, 0, 2), (Y2, 0, 0),
    (Z1, 1, 1), (Y2, 1, 0), (Z1, 2, 1), (Z1, 3, 1), (Y2, 2, 0), (Z1, 4, 1), (Z1, 5, 1), (Y2, 0, 1), (Z1, 6, 1),
    (Z1, 0, 3), (Z1, 1, 2), (Z1, 2, 2), (Z1, 3, 2), (Y2, 1, 1), (Z1, 4, 2), (Z1, 5, 2), (Z1, 6, 2), (Z1, 0, 4),
    (Z1, 1, 3), (Y2, 2, 1), (Z1, 2, 3), (Z1, 3, 3), (Y2, 0, 2), (Z1, 4, 3), (Z1, 5, 3), (Y2, 1, 2), (Z1, 6, 3),
    (Z1, 1, 4), (Z1, 2, 4), (Z1, 3, 4), (Y2, 2, 2), (Z1, 4, 4), (Z1, 5, 4), (Z1, 6, 4),
)


def fixed_tables():
    n = np.arange(NFFT)
    taper = 0.5 - 0.5 * np.cos(2.0 * np.pi / NFFT * n)
    bins = (np.arange(FQ)[:, None] + FQ * np.arange(NT)[None, :]).reshape(-1)
    angle = 2.0 * np.pi / NFFT * (bins[:, None] * n[None, :] % NFFT)
    return np.stack([taper * np.cos(angle), taper * np.sin(angle)]).astype(np.float32)


def dot_nt(left, right):
    return lax.dot_general(left, right, (((1,), (1,)), ((), ())), preferred_element_type=jnp.float32)


def kernel(
    x_hbm, fixed_hbm, dead_hbm, source_hbm, start_ref, out_ref,
    x_ref, fixed, dead_ref, source_ref, table_ref, sel_ref, spec, raw, sums,
    part, parts_in, line, lines_in, common, send, band, mats, g1, g2,
    in_sem, ps_send, ps_recv, re_send, re_recv, s1, r1, s2, r2,
):
    chan, tm = lax.axis_index("chan"), lax.axis_index("tm")
    y, z = chan // NZ, chan % NZ

    def at_y(step):
        return {"chan": (y + step + NY) % NY * NZ + z}

    def at_z(step):
        return {"chan": y * NZ + (z + step + NZ) % NZ}

    def at_t(step):
        return {"tm": (tm + step) % NT}

    def remote(src, dst, send_sem, recv_sem, where):
        return pltpu.make_async_remote_copy(
            src_ref=src, dst_ref=dst, send_sem=send_sem, recv_sem=recv_sem,
            device_id=where, device_id_type=pl.DeviceIdType.MESH,
        )

    sent = {}

    def start(key, *args):
        copy = remote(*args)
        copy.start()
        sent.setdefault(key, []).append(copy)

    def settle(key):
        for copy in sent.pop(key, []):
            copy.wait_send()

    def arrived(ref, sem):
        pltpu.make_async_copy(ref, ref, sem).wait()

    fetches = [
        pltpu.make_async_copy(dead_hbm, dead_ref, in_sem.at[0]),
        pltpu.make_async_copy(source_hbm, source_ref, in_sem.at[1]),
        pltpu.make_async_copy(fixed_hbm, fixed, in_sem.at[2]),
    ]
    quarter = NT * NFFT // 4
    for k in range(4):
        part_of = slice(k * quarter, (k + 1) * quarter)
        fetches.append(pltpu.make_async_copy(x_hbm.at[:, part_of], x_ref.at[:, part_of], in_sem.at[3 + k]))
    for fetch in fetches:
        fetch.start()

    barrier = pltpu.get_barrier_semaphore()
    for peer in (
        [at_z(s) for s in range(1, NZ)] + [at_y(s) for s in range(1, NY)] + [at_t(s) for s in range(1, NT)]
    ):
        pl.semaphore_signal(barrier, inc=1, device_id=peer, device_id_type=pl.DeviceIdType.MESH)

    for k in range(2):
        fetches[k].wait()
    phase = start_ref[0] * lax.broadcasted_iota(jnp.int32, (8, NFFT), 1) % NFFT
    angle = 2.0 * jnp.pi / NFFT * phase.astype(jnp.float32)
    shift_cos = jnp.concatenate([jnp.cos(angle)] * 2, axis=0)
    shift_sin = jnp.concatenate([jnp.sin(angle)] * 2, axis=0)
    ids = chan * CH + lax.broadcasted_iota(jnp.int32, (8, CH), 1)

    def strike(step, mask):
        for k in range(8):
            mask = jnp.where(ids == dead_ref[8 * step + k], 0.0, mask)
        return mask

    live = lax.fori_loop(0, DEAD // 8, strike, jnp.ones((8, CH), jnp.float32))
    live_rows = jnp.broadcast_to(live[0:1], (CH, CH)).T
    live_rows = jnp.concatenate([live_rows, live_rows], axis=1)
    source_ids = chan * CH + lax.broadcasted_iota(jnp.int32, (SRC, CH), 1)
    source_rows = lax.broadcasted_iota(jnp.int32, (SRC, CH), 0)
    wanted = jnp.zeros((SRC, CH), jnp.int32)
    for k in range(SRC):
        wanted = jnp.where(source_rows == k, source_ref[k], wanted)
    sel_ref[...] = jnp.where(wanted == source_ids, 1.0, 0.0).astype(jnp.bfloat16)
    fetches[2].wait()
    for i in range(FQ):
        cos_i, sin_i = fixed[0, NT * i:NT * (i + 1)], fixed[1, NT * i:NT * (i + 1)]
        table_ref[32 * i:32 * i + 16] = (shift_cos * cos_i - shift_sin * sin_i).astype(jnp.bfloat16)
        table_ref[32 * i + 16:32 * i + 32] = (-(shift_sin * cos_i + shift_cos * sin_i)).astype(jnp.bfloat16)
    table_ref[ROWS:] = jnp.zeros((PAD - ROWS, NFFT), jnp.bfloat16)

    for k in range(4):
        fetches[3 + k].wait()
        blocks = [x_ref[:, (4 * k + b) * NFFT:(4 * k + b + 1) * NFFT] for b in range(4)]
        values = dot_nt(jnp.concatenate(blocks, axis=0), table_ref[...])
        for b in range(4):
            value = values[CH * b:CH * (b + 1)]
            spec[4 * k + b] = value
            sums[4 * k + b:4 * k + b + 1] = jnp.sum(value * live_rows, axis=0, keepdims=True)
    for q in range(3):
        lanes = slice(64 * q, 64 * q + 64)
        part[q] = jnp.concatenate([sums[0:8, lanes], sums[8:16, lanes]], axis=1)

    pl.semaphore_wait(barrier, (NZ - 1) + (NY - 1) + (NT - 1))

    pieces = (slice(0, 1), slice(1, 3))
    for n, piece in enumerate(pieces):
        for s in range(1, NZ):
            start(
                "sum", part.at[piece], parts_in.at[s - 1, piece],
                ps_send.at[n, s - 1], ps_recv.at[n, s - 1], at_z(s),
            )

    def turn(b, carry):
        to = pl.multiple_of(b * ROWS, ROWS)
        raw[pl.ds(to, CH), :] = spec[b, :, 0:CH].T
        raw[pl.ds(to + CH, ROWS - CH), :] = spec[b, :, CH:].T[0:ROWS - CH]
        return carry

    lax.fori_loop(0, NT // 2, turn, 0)
    for n, piece in enumerate(pieces):
        total = part[piece]
        for s in range(1, NZ):
            arrived(parts_in.at[s - 1, piece], ps_recv.at[n, s - 1])
            total = total + parts_in[s - 1, piece]
        line[piece] = total
        for s in range(1, NY):
            start(
                "sum", line.at[piece], lines_in.at[s - 1, piece],
                ps_send.at[n, 6 + s], ps_recv.at[n, 6 + s], at_y(s),
            )
    lax.fori_loop(NT // 2, NT, turn, 0)

    def close_sum(n):
        piece = pieces[n]
        total = line[piece]
        for s in range(1, NY):
            arrived(lines_in.at[s - 1, piece], ps_recv.at[n, 6 + s])
            total = total + lines_in[s - 1, piece]
        common[piece] = total / (NCHAN - DEAD)

    def give(group):
        first, last = GROUPS[group]
        for i in range(first, last):
            mode = common[i // 2]
            for p in range(2):
                for d in range(NT):
                    both = []
                    for half in range(2):
                        lane = 64 * half + 32 * (i % 2) + 16 * p + d
                        value = raw[pl.ds(8 * half * ROWS + 32 * i + 16 * p + d, 8, stride=ROWS), :]
                        both.append(live * (value - jnp.broadcast_to(mode[:, lane:lane + 1], (8, CH))))
                    send[i, d, p] = jnp.concatenate(both, axis=0).astype(jnp.bfloat16)
        for s in range(1, NT):
            remote(
                send.at[first:last, (tm + s) % NT], band.at[first:last, tm],
                re_send.at[group], re_recv.at[group], at_t(s),
            ).start()
        for i in range(first, last):
            band[i, tm] = send[i, tm]

    def whiten(i):
        real = band[i, :, 0].reshape(BLOCKS, CH).astype(jnp.float32)
        imag = band[i, :, 1].reshape(BLOCKS, CH).astype(jnp.float32)
        power = jnp.sum(real * real + imag * imag, axis=0, keepdims=True) / BLOCKS
        scale = lax.rsqrt(power + EPS)
        real, imag = real * scale, imag * scale
        mats[i, 0:BLOCKS, 0:CH] = real.astype(jnp.bfloat16)
        mats[i, BLOCKS:, 0:CH] = imag.astype(jnp.bfloat16)
        mats[i, 0:BLOCKS, CH:] = imag.astype(jnp.bfloat16)
        mats[i, BLOCKS:, CH:] = (-real).astype(jnp.bfloat16)
        rows = dot_nt(sel_ref[...], mats[i, :, 0:CH]).astype(jnp.bfloat16)
        for h in range(2):
            kind, u = UNITS[(i, h)]
            piece = rows[HALF * h:HALF * (h + 1)]
            if kind == 1:
                g1[u, z, 0] = piece
            else:
                g2[u, y, z] = piece

    def first_y(u, stage):
        if stage == 0:
            mine = g1.at[u, z, 0]
            start((Y1, u), mine, g1.at[u, z, 3], s1.at[u, 0], r1.at[u, 0], at_y(1))
            start((Y1, u), mine, g1.at[u, z, 1], s1.at[u, 1], r1.at[u, 1], at_y(-1))
        else:
            arrived(g1.at[u, z, 3], r1.at[u, 0])
            arrived(g1.at[u, z, 1], r1.at[u, 1])
            if u % 2 == 0:
                start((Y1, u), g1.at[u, z, 3], g1.at[u, z, 2], s1.at[u, 2], r1.at[u, 2], at_y(1))
            else:
                start((Y1, u), g1.at[u, z, 1], g1.at[u, z, 2], s1.at[u, 2], r1.at[u, 2], at_y(-1))

    def own_z(u, stage):
        left, right = (z - stage + NZ) % NZ, (z + stage) % NZ
        if 0 < stage < 4:
            arrived(g1.at[u, left, 0], r1.at[u, 9 + 2 * stage])
            arrived(g1.at[u, right, 0], r1.at[u, 10 + 2 * stage])
        if stage == 4:
            arrived(g1.at[u, left, 0], r1.at[u, 17])
            return
        a, b = g1.at[u, left, 0], g1.at[u, right, 0]
        if stage < 3 or u % 2 == 1:
            to = 17 if stage == 3 else 11 + 2 * stage
            start((OWN1, u), a, a, s1.at[u, to], r1.at[u, to], at_z(1))
        if stage < 3 or u % 2 == 0:
            to = 17 if stage == 3 else 12 + 2 * stage
            start((OWN1, u), b, b, s1.at[u, to], r1.at[u, to], at_z(-1))

    def then_z(u, stage):
        low = 1 if u in EARLY else 0
        middle = 2 if low == 0 or u % 2 == 1 else 3
        left, right = (z - stage + NZ) % NZ, (z + stage) % NZ
        if stage == 0:
            arrived(g1.at[u, z, 2], r1.at[u, 2])
        elif stage < 4:
            arrived(g1.at[u, left, low:4], r1.at[u, 1 + 2 * stage])
            arrived(g1.at[u, right, low:4], r1.at[u, 2 + 2 * stage])
        else:
            arrived(g1.at[u, left, low:middle], r1.at[u, 9])
            arrived(g1.at[u, left, middle:4], r1.at[u, 10])
            if low:
                own_z(u, 4)
            lines(u, (4,))
            return
        if stage < 3:
            a, b = g1.at[u, left, low:4], g1.at[u, right, low:4]
        else:
            a, b = g1.at[u, left, low:middle], g1.at[u, right, middle:4]
        start((Z1, u, stage == 3), a, a, s1.at[u, 3 + 2 * stage], r1.at[u, 3 + 2 * stage], at_z(1))
        start((Z1, u, stage == 3), b, b, s1.at[u, 4 + 2 * stage], r1.at[u, 4 + 2 * stage], at_z(-1))
        if stage == 3:
            for steps in ((-3, -2, -1, 0), (1, 2, 3)):
                lines(u, steps)
            for key in ((Y1, u), (OWN1, u), (Z1, u, False)):
                settle(key)

    def lines(u, steps):
        i, h = PLACE[(1, u)]
        at = [(z + step + NZ) % NZ for step in steps]
        left = jnp.concatenate([g1[u, zz].reshape(NY * HALF, 2 * BLOCKS) for zz in at], axis=0)
        both = jnp.dot(left, mats[i], preferred_element_type=jnp.float32) * (1.0 / BLOCKS)
        both = both.astype(jnp.bfloat16).reshape(len(steps), NY, HALF, 2 * CH)
        for k, zz in enumerate(at):
            for up in range(NY):
                out_ref[0, i, (y + up) % NY, zz, h] = both[k, up, :, 0:CH]
                out_ref[1, i, (y + up) % NY, zz, h] = both[k, up, :, CH:]

    def first_z(u, stage):
        left, right = (z - stage + NZ) % NZ, (z + stage) % NZ
        if stage > 0:
            arrived(g2.at[u, y, left], r2.at[u, 2 * stage - 2])
            arrived(g2.at[u, y, right], r2.at[u, 2 * stage - 1])
        a, b = g2.at[u, y, left], g2.at[u, y, right]
        if stage < 3 or u % 2 == 0:
            start((Z2, u), a, a, s2.at[u, 2 * stage], r2.at[u, 2 * stage], at_z(1))
        if stage < 3 or u % 2 == 1:
            start((Z2, u), b, b, s2.at[u, 2 * stage + 1], r2.at[u, 2 * stage + 1], at_z(-1))

    def then_y(u, stage):
        down, up, far = (y - 1 + NY) % NY, (y + 1) % NY, (y + 2) % NY
        if stage == 0:
            arrived(g2.at[u, y, (z + 4) % NZ], r2.at[u, 6 + u % 2])
            start((Y2, u, 0), g2.at[u, y], g2.at[u, y], s2.at[u, 8], r2.at[u, 8], at_y(1))
            start((Y2, u, 0), g2.at[u, y], g2.at[u, y], s2.at[u, 9], r2.at[u, 9], at_y(-1))
        elif stage == 1:
            arrived(g2.at[u, down], r2.at[u, 8])
            arrived(g2.at[u, up], r2.at[u, 9])
            a, b = g2.at[u, down, 0:4], g2.at[u, up, 4:8]
            start((Y2, u, 1), a, a, s2.at[u, 10], r2.at[u, 10], at_y(1))
            start((Y2, u, 1), b, b, s2.at[u, 11], r2.at[u, 11], at_y(-1))
            columns(u, (-1, 0, 1))
            settle((Z2, u))
        else:
            arrived(g2.at[u, far, 0:4], r2.at[u, 10])
            arrived(g2.at[u, far, 4:8], r2.at[u, 11])
            columns(u, (2,))
            settle((Y2, u, 0))

    def columns(u, steps):
        i, h = PLACE[(2, u)]
        at = [(y + step + NY) % NY for step in steps]
        left = jnp.concatenate([g2[u, yy].reshape(NZ * HALF, 2 * BLOCKS) for yy in at], axis=0)
        both = jnp.dot(left, mats[i], preferred_element_type=jnp.float32) * (1.0 / BLOCKS)
        both = both.astype(jnp.bfloat16).reshape(len(steps), NZ, HALF, 2 * CH)
        for k, yy in enumerate(at):
            out_ref[0, i, yy, :, h] = both[k, :, :, 0:CH]
            out_ref[1, i, yy, :, h] = both[k, :, :, CH:]

    def take(group):
        first, last = GROUPS[group]
        arrived(band.at[first:last, 0:NT - 1], re_recv.at[group])
        for i in range(first, last):
            whiten(i)

    def free(group):
        first, last = GROUPS[group]
        arrived(send.at[first:last, 0:NT - 1], re_send.at[group])

    steps = (take, first_y, then_z, own_z, first_z, then_y)
    close_sum(0)
    give(0)
    close_sum(1)
    give(1)
    for at, (step, unit, stage) in enumerate(ORDER):
        if at == LATE:
            give(2)
        if at == LATE + 44:
            settle("sum")
            for group in range(len(GROUPS)):
                free(group)
        if step == TAKE:
            take(unit)
        else:
            steps[step](unit, stage)
    for key in list(sent):
        settle(key)


def body(strain_record, dead_channels, source_channels, band_start):
    vmem = pl.BlockSpec(memory_space=pltpu.VMEM)
    hbm = pl.BlockSpec(memory_space=pltpu.HBM)
    dma = pltpu.SemaphoreType.DMA
    out = pl.pallas_call(
        kernel,
        out_shape=jax.ShapeDtypeStruct((2, FQ, NY, NZ, 2, HALF, CH), jnp.bfloat16),
        in_specs=[hbm] * 4 + [pl.BlockSpec(memory_space=pltpu.SMEM)],
        out_specs=vmem,
        scratch_shapes=[
            pltpu.VMEM((CH, NT * NFFT), jnp.bfloat16),
            pltpu.VMEM((2, FQ * NT, NFFT), jnp.float32),
            pltpu.SMEM((DEAD,), jnp.int32),
            pltpu.SMEM((SRC,), jnp.int32),
            pltpu.VMEM((PAD, NFFT), jnp.bfloat16),
            pltpu.VMEM((SRC, CH), jnp.bfloat16),
            pltpu.VMEM((NT, CH, PAD), jnp.float32),
            pltpu.VMEM((NT * ROWS, CH), jnp.float32),
            pltpu.VMEM((NT, PAD), jnp.float32),
            pltpu.VMEM((3, 8, CH), jnp.float32),
            pltpu.VMEM((NZ - 1, 3, 8, CH), jnp.float32),
            pltpu.VMEM((3, 8, CH), jnp.float32),
            pltpu.VMEM((NY - 1, 3, 8, CH), jnp.float32),
            pltpu.VMEM((3, 8, CH), jnp.float32),
            pltpu.VMEM((FQ, NT, 2, NT, CH), jnp.bfloat16),
            pltpu.VMEM((FQ, NT, 2, NT, CH), jnp.bfloat16),
            pltpu.VMEM((FQ, 2 * BLOCKS, 2 * CH), jnp.bfloat16),
            pltpu.VMEM((NP1, NZ, NY, HALF, 2 * BLOCKS), jnp.bfloat16),
            pltpu.VMEM((NP2, NY, NZ, HALF, 2 * BLOCKS), jnp.bfloat16),
            dma((7,)), dma((2, 10)), dma((2, 10)), dma((3,)), dma((3,)),
            dma((NP1, 18)), dma((NP1, 18)), dma((NP2, 12)), dma((NP2, 12)),
        ],
        compiler_params=pltpu.CompilerParams(
            collective_id=0, has_side_effects=True, vmem_limit_bytes=48 * 1024 * 1024
        ),
    )(*[
        pltpu.with_memory_space_constraint(array, pltpu.HBM)
        for array in (strain_record, jnp.asarray(fixed_tables()), dead_channels, source_channels)
    ], band_start)
    return out.reshape(2, FQ, NY * NZ * SRC, CH)


def solution(mesh):
    in_specs = (P("chan", "tm"), P(), P("chan"), P())
    out_specs = P(None, "tm", None, "chan")
    return jax.shard_map(body, mesh=mesh, in_specs=in_specs, out_specs=out_specs, check_vma=False)
```

```python
import jax
import jax.numpy as jnp
import numpy as np
from jax import lax
from jax.experimental import pallas as pl
from jax.experimental.pallas import tpu as pltpu
from jax.sharding import PartitionSpec as P

NFFT = 512
FQ = 5
NT = 16
NY, NZ = 4, 8
CH = 128
SRC = 32
HALF = 16
NCHAN = NY * NZ * CH
BLOCKS = 256
DEAD = 200
ROWS = 2 * FQ * NT
PAD = 256
EPS = 1e-06
FAR_FIRST = (4, 3, 5, 12, 11, 13, 2, 6, 10, 14, 8, 7, 9, 1, 15)
NP1, NP2 = 7, 3

UNITS = {(0, 0): (2, 0), (0, 1): (1, 0), (1, 0): (2, 1), (1, 1): (1, 1), (2, 0): (2, 2), (2, 1): (1, 2), (3, 0): (1, 3), (3, 1): (1, 4), (4, 0): (1, 5), (4, 1): (1, 6)}
PLACE = {unit: at for at, unit in UNITS.items()}
EARLY = (0, 1, 2)
GROUPS = ((0, 1), (1, 3), (3, 5))
LATE = 4
TAKE, Y1, Z1, OWN1, Z2, Y2 = range(6)
ORDER = (
    (TAKE, 0, 0), (OWN1, 0, 0), (Y1, 0, 0), (Z2, 0, 0), (TAKE, 1, 0), (OWN1, 1, 0), (Y1, 1, 0), (Z2, 1, 0),
    (OWN1, 2, 0), (Y1, 2, 0), (Z2, 2, 0), (OWN1, 0, 1), (Y1, 0, 1), (Z2, 0, 1), (OWN1, 1, 1), (TAKE, 2, 0),
    (Y1, 3, 0), (Y1, 4, 0), (Y1, 5, 0), (Y1, 6, 0), (Y1, 1, 1), (Z2, 1, 1), (OWN1, 2, 1), (Y1, 2, 1), (Z2, 2, 1),
    (OWN1, 0, 2), (Z1, 0, 0), (Z2, 0, 2), (OWN1, 1, 2), (Z2, 1, 2), (Y1, 3, 1), (OWN1, 2, 2), (Z2, 2, 2),
    (Y1, 4, 1), (OWN1, 0, 3), (Y1, 5, 1), (Z1, 0, 1), (Y1, 6, 1), (Z2, 0, 3), (OWN1, 1, 3), (Z1, 1, 0), (Z1, 2, 0),
    (Z2, 1, 3), (OWN1, 2, 3), (Z1, 3, 0), (Z2, 2, 3), (Z1, 4, 0), (Z1, 5, 0), (Z1, 6, 0), (Z1, 0, 2), (Y2, 0, 0),
    (Z1, 1, 1), (Y2, 1, 0), (Z1, 2, 1), (Z1, 3, 1), (Y2, 2, 0), (Z1, 4, 1), (Z1, 5, 1), (Y2, 0, 1), (Z1, 6, 1),
    (Z1, 0, 3), (Z1, 1, 2), (Z1, 2, 2), (Z1, 3, 2), (Y2, 1, 1), (Z1, 4, 2), (Z1, 5, 2), (Z1, 6, 2), (Z1, 0, 4),
    (Z1, 1, 3), (Y2, 2, 1), (Z1, 2, 3), (Z1, 3, 3), (Y2, 0, 2), (Z1, 4, 3), (Z1, 5, 3), (Y2, 1, 2), (Z1, 6, 3),
    (Z1, 1, 4), (Z1, 2, 4), (Z1, 3, 4), (Y2, 2, 2), (Z1, 4, 4), (Z1, 5, 4), (Z1, 6, 4),
)


def fixed_tables():
    n = np.arange(NFFT)
    taper = 0.5 - 0.5 * np.cos(2.0 * np.pi / NFFT * n)
    bins = (np.arange(FQ)[:, None] + FQ * np.arange(NT)[None, :]).reshape(-1)
    angle = 2.0 * np.pi / NFFT * (bins[:, None] * n[None, :] % NFFT)
    return np.stack([taper * np.cos(angle), taper * np.sin(angle)]).astype(np.float32)


def dot_nt(left, right):
    return lax.dot_general(left, right, (((1,), (1,)), ((), ())), preferred_element_type=jnp.float32)


def kernel(
    x_hbm, fixed_hbm, dead_hbm, source_hbm, start_ref, out_ref,
    x_ref, fixed, dead_ref, source_ref, table_ref, sel_ref, raw, sums,
    part, parts_in, line, lines_in, common, send, band, mats, g1, g2,
    in_sem, ps_send, ps_recv, re_send, re_recv, s1, r1, s2, r2,
):
    chan, tm = lax.axis_index("chan"), lax.axis_index("tm")
    y, z = lax.div(chan, NZ), lax.rem(chan, NZ)

    ys = [lax.rem(y + step, NY) for step in range(NY)]
    zs = [lax.rem(z + step, NZ) for step in range(NZ)]
    ts = [lax.rem(tm + step, NT) for step in range(NT)]
    along_y = [(ys[step] * NZ + z, tm) for step in range(NY)]
    along_z = [(y * NZ + zs[step], tm) for step in range(NZ)]

    def at_y(step):
        return along_y[step % NY]

    def at_z(step):
        return along_z[step % NZ]

    def at_t(step):
        return (chan, ts[step % NT])

    def remote(src, dst, send_sem, recv_sem, where):
        return pltpu.make_async_remote_copy(
            src_ref=src, dst_ref=dst, send_sem=send_sem, recv_sem=recv_sem,
            device_id=where, device_id_type=pl.DeviceIdType.MESH,
        )

    sent = {}

    def start(key, *args):
        copy = remote(*args)
        copy.start()
        sent.setdefault(key, []).append(copy)

    def settle(key):
        for copy in sent.pop(key, []):
            copy.wait_send()

    def arrived(ref, sem):
        pltpu.make_async_copy(ref, ref, sem).wait()

    fetches = [
        pltpu.make_async_copy(dead_hbm, dead_ref, in_sem.at[0]),
        pltpu.make_async_copy(source_hbm, source_ref, in_sem.at[1]),
        pltpu.make_async_copy(fixed_hbm, fixed, in_sem.at[2]),
    ]
    quarter = NT * NFFT // 4
    for k in range(4):
        part_of = slice(k * quarter, (k + 1) * quarter)
        fetches.append(pltpu.make_async_copy(x_hbm.at[:, part_of], x_ref.at[:, part_of], in_sem.at[3 + k]))
    for fetch in fetches:
        fetch.start()

    barrier = pltpu.get_barrier_semaphore()
    for peer in (
        [at_z(s) for s in range(1, NZ)] + [at_y(s) for s in range(1, NY)] + [at_t(s) for s in range(1, NT)]
    ):
        pl.semaphore_signal(barrier, inc=1, device_id=peer, device_id_type=pl.DeviceIdType.MESH)

    for k in range(2):
        fetches[k].wait()
    phase = start_ref[0] * lax.broadcasted_iota(jnp.int32, (8, NFFT), 1) % NFFT
    angle = 2.0 * jnp.pi / NFFT * phase.astype(jnp.float32)
    shift_cos = jnp.concatenate([jnp.cos(angle)] * 2, axis=0)
    shift_sin = jnp.concatenate([jnp.sin(angle)] * 2, axis=0)
    ids = chan * CH + lax.broadcasted_iota(jnp.int32, (8, CH), 1)

    def strike(step, mask):
        for k in range(8):
            mask = jnp.where(ids == dead_ref[8 * step + k], 0.0, mask)
        return mask

    live = lax.fori_loop(0, DEAD // 8, strike, jnp.ones((8, CH), jnp.float32))
    live_rows = jnp.broadcast_to(live[0:1], (CH, CH)).T
    live_rows = jnp.concatenate([live_rows, live_rows], axis=1)
    fetches[2].wait()
    for i in range(FQ):
        cos_i, sin_i = fixed[0, NT * i:NT * (i + 1)], fixed[1, NT * i:NT * (i + 1)]
        table_ref[32 * i:32 * i + 16] = (shift_cos * cos_i - shift_sin * sin_i).astype(jnp.bfloat16)
        table_ref[32 * i + 16:32 * i + 32] = (-(shift_sin * cos_i + shift_cos * sin_i)).astype(jnp.bfloat16)
    table_ref[ROWS:] = jnp.zeros((PAD - ROWS, NFFT), jnp.bfloat16)

    for k in range(4):
        fetches[3 + k].wait()
        blocks = [x_ref[:, (4 * k + b) * NFFT:(4 * k + b + 1) * NFFT] for b in range(4)]
        values = dot_nt(jnp.concatenate(blocks, axis=0), table_ref[...])
        for b in range(4):
            value = values[CH * b:CH * (b + 1)]
            sums[4 * k + b:4 * k + b + 1] = jnp.sum(value * live_rows, axis=0, keepdims=True)
    for q in range(3):
        lanes = slice(64 * q, 64 * q + 64)
        part[q] = jnp.concatenate([sums[0:8, lanes], sums[8:16, lanes]], axis=1)

    pl.semaphore_wait(barrier, (NZ - 1) + (NY - 1) + (NT - 1))

    pieces = (slice(0, 1), slice(1, 3))

    def sum_z(n):
        for s in range(1, NZ):
            start(
                "sum", part.at[pieces[n]], parts_in.at[s - 1, pieces[n]],
                ps_send.at[n, s - 1], ps_recv.at[n, s - 1], at_z(s),
            )

    def sum_y(n):
        total = part[pieces[n]]
        for s in range(1, NZ):
            arrived(parts_in.at[s - 1, pieces[n]], ps_recv.at[n, s - 1])
            total = total + parts_in[s - 1, pieces[n]]
        line[pieces[n]] = total
        for s in range(1, NY):
            start(
                "sum", line.at[pieces[n]], lines_in.at[s - 1, pieces[n]],
                ps_send.at[n, 6 + s], ps_recv.at[n, 6 + s], at_y(s),
            )

    def close_sum(n):
        total = line[pieces[n]]
        for s in range(1, NY):
            arrived(lines_in.at[s - 1, pieces[n]], ps_recv.at[n, 6 + s])
            total = total + lines_in[s - 1, pieces[n]]
        common[pieces[n]] = total / (NCHAN - DEAD)

    def transform(b, carry):
        samples = x_ref[:, pl.ds(pl.multiple_of(b * NFFT, NFFT), NFFT)]
        raw[pl.ds(b, ROWS, stride=NT), :] = dot_nt(table_ref[0:ROWS], samples)
        return carry

    sum_z(0)
    sum_z(1)
    source_ids = chan * CH + lax.broadcasted_iota(jnp.int32, (SRC, CH), 1)
    source_rows = lax.broadcasted_iota(jnp.int32, (SRC, CH), 0)
    wanted = jnp.zeros((SRC, CH), jnp.int32)
    for k in range(SRC):
        wanted = jnp.where(source_rows == k, source_ref[k], wanted)
    sel_ref[...] = jnp.where(wanted == source_ids, 1.0, 0.0).astype(jnp.bfloat16)
    lax.fori_loop(0, NT // 2, transform, 0)
    sum_y(0)
    sum_y(1)
    lax.fori_loop(NT // 2, NT, transform, 0)

    def give(group):
        first, last = GROUPS[group]
        for i in range(first, last):
            mode = common[i // 2]
            for p in range(2):
                for d in range(NT):
                    both = []
                    for half in range(2):
                        lane = 64 * half + 32 * (i % 2) + 16 * p + d
                        row = NT * (32 * i + 16 * p + d) + 8 * half
                        value = raw[row:row + 8]
                        both.append(live * (value - jnp.broadcast_to(mode[:, lane:lane + 1], (8, CH))))
                    send[i, d, p] = jnp.concatenate(both, axis=0).astype(jnp.bfloat16)
        for s in FAR_FIRST:
            remote(
                send.at[first:last, ts[s]], band.at[first:last, tm],
                re_send.at[group], re_recv.at[group], at_t(s),
            ).start()
        for i in range(first, last):
            band[i, tm] = send[i, tm]

    def whiten(i):
        real = band[i, :, 0].reshape(BLOCKS, CH).astype(jnp.float32)
        imag = band[i, :, 1].reshape(BLOCKS, CH).astype(jnp.float32)
        power = jnp.sum(real * real + imag * imag, axis=0, keepdims=True) / BLOCKS
        scale = lax.rsqrt(power + EPS)
        real, imag = real * scale, imag * scale
        mats[i, 0:BLOCKS, 0:CH] = real.astype(jnp.bfloat16)
        mats[i, BLOCKS:, 0:CH] = imag.astype(jnp.bfloat16)
        mats[i, 0:BLOCKS, CH:] = imag.astype(jnp.bfloat16)
        mats[i, BLOCKS:, CH:] = (-real).astype(jnp.bfloat16)
        rows = dot_nt(sel_ref[...], mats[i, :, 0:CH]).astype(jnp.bfloat16)
        for h in range(2):
            kind, u = UNITS[(i, h)]
            piece = rows[HALF * h:HALF * (h + 1)]
            if kind == 1:
                g1[u, z, 0] = piece
            else:
                g2[u, y, z] = piece

    def first_y(u, stage):
        if stage == 0:
            mine = g1.at[u, z, 0]
            start((Y1, u), mine, g1.at[u, z, 3], s1.at[u, 0], r1.at[u, 0], at_y(1))
            start((Y1, u), mine, g1.at[u, z, 1], s1.at[u, 1], r1.at[u, 1], at_y(-1))
        else:
            arrived(g1.at[u, z, 3], r1.at[u, 0])
            arrived(g1.at[u, z, 1], r1.at[u, 1])
            if u % 2 == 0:
                start((Y1, u), g1.at[u, z, 3], g1.at[u, z, 2], s1.at[u, 2], r1.at[u, 2], at_y(1))
            else:
                start((Y1, u), g1.at[u, z, 1], g1.at[u, z, 2], s1.at[u, 2], r1.at[u, 2], at_y(-1))

    def own_z(u, stage):
        left, right = zs[-stage % NZ], zs[stage]
        if 0 < stage < 4:
            arrived(g1.at[u, left, 0], r1.at[u, 9 + 2 * stage])
            arrived(g1.at[u, right, 0], r1.at[u, 10 + 2 * stage])
        if stage == 4:
            arrived(g1.at[u, left, 0], r1.at[u, 17])
            return
        a, b = g1.at[u, left, 0], g1.at[u, right, 0]
        if stage < 3 or u % 2 == 1:
            to = 17 if stage == 3 else 11 + 2 * stage
            start((OWN1, u), a, a, s1.at[u, to], r1.at[u, to], at_z(1))
        if stage < 3 or u % 2 == 0:
            to = 17 if stage == 3 else 12 + 2 * stage
            start((OWN1, u), b, b, s1.at[u, to], r1.at[u, to], at_z(-1))

    def then_z(u, stage):
        low = 1 if u in EARLY else 0
        middle = 2 if low == 0 or u % 2 == 1 else 3
        left, right = zs[-stage % NZ], zs[stage]
        if stage == 0:
            arrived(g1.at[u, z, 2], r1.at[u, 2])
        elif stage < 4:
            arrived(g1.at[u, left, low:4], r1.at[u, 1 + 2 * stage])
            arrived(g1.at[u, right, low:4], r1.at[u, 2 + 2 * stage])
        else:
            arrived(g1.at[u, left, low:middle], r1.at[u, 9])
            arrived(g1.at[u, left, middle:4], r1.at[u, 10])
            if low:
                own_z(u, 4)
            lines(u, (4,))
            return
        if stage < 3:
            a, b = g1.at[u, left, low:4], g1.at[u, right, low:4]
        else:
            a, b = g1.at[u, left, low:middle], g1.at[u, right, middle:4]
        start((Z1, u, stage == 3), a, a, s1.at[u, 3 + 2 * stage], r1.at[u, 3 + 2 * stage], at_z(1))
        start((Z1, u, stage == 3), b, b, s1.at[u, 4 + 2 * stage], r1.at[u, 4 + 2 * stage], at_z(-1))
        if stage == 3:
            for steps in ((-3, -2, -1, 0), (1, 2, 3)):
                lines(u, steps)
            for key in ((Y1, u), (OWN1, u), (Z1, u, False)):
                settle(key)

    def lines(u, steps):
        i, h = PLACE[(1, u)]
        at = [zs[step % NZ] for step in steps]
        left = jnp.concatenate([g1[u, zz].reshape(NY * HALF, 2 * BLOCKS) for zz in at], axis=0)
        both = jnp.dot(left, mats[i], preferred_element_type=jnp.float32) * (1.0 / BLOCKS)
        both = both.astype(jnp.bfloat16).reshape(len(steps), NY, HALF, 2 * CH)
        for k, zz in enumerate(at):
            for up in range(NY):
                out_ref[0, i, ys[up], zz, h] = both[k, up, :, 0:CH]
                out_ref[1, i, ys[up], zz, h] = both[k, up, :, CH:]

    def first_z(u, stage):
        left, right = zs[-stage % NZ], zs[stage]
        if stage > 0:
            arrived(g2.at[u, y, left], r2.at[u, 2 * stage - 2])
            arrived(g2.at[u, y, right], r2.at[u, 2 * stage - 1])
        a, b = g2.at[u, y, left], g2.at[u, y, right]
        if stage < 3 or u % 2 == 0:
            start((Z2, u), a, a, s2.at[u, 2 * stage], r2.at[u, 2 * stage], at_z(1))
        if stage < 3 or u % 2 == 1:
            start((Z2, u), b, b, s2.at[u, 2 * stage + 1], r2.at[u, 2 * stage + 1], at_z(-1))

    def then_y(u, stage):
        down, up, far = ys[3], ys[1], ys[2]
        if stage == 0:
            arrived(g2.at[u, y, zs[4]], r2.at[u, 6 + u % 2])
            start((Y2, u, 0), g2.at[u, y], g2.at[u, y], s2.at[u, 8], r2.at[u, 8], at_y(1))
            start((Y2, u, 0), g2.at[u, y], g2.at[u, y], s2.at[u, 9], r2.at[u, 9], at_y(-1))
        elif stage == 1:
            arrived(g2.at[u, down], r2.at[u, 8])
            arrived(g2.at[u, up], r2.at[u, 9])
            a, b = g2.at[u, down, 0:4], g2.at[u, up, 4:8]
            start((Y2, u, 1), a, a, s2.at[u, 10], r2.at[u, 10], at_y(1))
            start((Y2, u, 1), b, b, s2.at[u, 11], r2.at[u, 11], at_y(-1))
            columns(u, (-1, 0, 1))
            settle((Z2, u))
        else:
            arrived(g2.at[u, far, 0:4], r2.at[u, 10])
            arrived(g2.at[u, far, 4:8], r2.at[u, 11])
            columns(u, (2,))
            settle((Y2, u, 0))

    def columns(u, steps):
        i, h = PLACE[(2, u)]
        at = [ys[step % NY] for step in steps]
        left = jnp.concatenate([g2[u, yy].reshape(NZ * HALF, 2 * BLOCKS) for yy in at], axis=0)
        both = jnp.dot(left, mats[i], preferred_element_type=jnp.float32) * (1.0 / BLOCKS)
        both = both.astype(jnp.bfloat16).reshape(len(steps), NZ, HALF, 2 * CH)
        for k, yy in enumerate(at):
            out_ref[0, i, yy, :, h] = both[k, :, :, 0:CH]
            out_ref[1, i, yy, :, h] = both[k, :, :, CH:]

    def take(group):
        first, last = GROUPS[group]
        arrived(band.at[first:last, 0:NT - 1], re_recv.at[group])
        for i in range(first, last):
            whiten(i)

    def free(group):
        first, last = GROUPS[group]
        arrived(send.at[first:last, 0:NT - 1], re_send.at[group])

    steps = (take, first_y, then_z, own_z, first_z, then_y)
    close_sum(0)
    give(0)
    close_sum(1)
    give(1)
    for at, (step, unit, stage) in enumerate(ORDER):
        if at == LATE:
            give(2)
        if at == LATE + 44:
            settle("sum")
            for group in range(len(GROUPS)):
                free(group)
        if step == TAKE:
            take(unit)
        else:
            steps[step](unit, stage)
    for key in list(sent):
        settle(key)


def body(strain_record, dead_channels, source_channels, band_start):
    vmem = pl.BlockSpec(memory_space=pltpu.VMEM)
    hbm = pl.BlockSpec(memory_space=pltpu.HBM)
    dma = pltpu.SemaphoreType.DMA
    out = pl.pallas_call(
        kernel,
        out_shape=jax.ShapeDtypeStruct((2, FQ, NY, NZ, 2, HALF, CH), jnp.bfloat16),
        in_specs=[hbm] * 4 + [pl.BlockSpec(memory_space=pltpu.SMEM)],
        out_specs=vmem,
        scratch_shapes=[
            pltpu.VMEM((CH, NT * NFFT), jnp.bfloat16),
            pltpu.VMEM((2, FQ * NT, NFFT), jnp.float32),
            pltpu.SMEM((DEAD,), jnp.int32),
            pltpu.SMEM((SRC,), jnp.int32),
            pltpu.VMEM((PAD, NFFT), jnp.bfloat16),
            pltpu.VMEM((SRC, CH), jnp.bfloat16),
            pltpu.VMEM((NT * ROWS, CH), jnp.float32),
            pltpu.VMEM((NT, PAD), jnp.float32),
            pltpu.VMEM((3, 8, CH), jnp.float32),
            pltpu.VMEM((NZ - 1, 3, 8, CH), jnp.float32),
            pltpu.VMEM((3, 8, CH), jnp.float32),
            pltpu.VMEM((NY - 1, 3, 8, CH), jnp.float32),
            pltpu.VMEM((3, 8, CH), jnp.float32),
            pltpu.VMEM((FQ, NT, 2, NT, CH), jnp.bfloat16),
            pltpu.VMEM((FQ, NT, 2, NT, CH), jnp.bfloat16),
            pltpu.VMEM((FQ, 2 * BLOCKS, 2 * CH), jnp.bfloat16),
            pltpu.VMEM((NP1, NZ, NY, HALF, 2 * BLOCKS), jnp.bfloat16),
            pltpu.VMEM((NP2, NY, NZ, HALF, 2 * BLOCKS), jnp.bfloat16),
            dma((7,)), dma((2, 10)), dma((2, 10)), dma((3,)), dma((3,)),
            dma((NP1, 18)), dma((NP1, 18)), dma((NP2, 12)), dma((NP2, 12)),
        ],
        compiler_params=pltpu.CompilerParams(
            collective_id=0, has_side_effects=True, vmem_limit_bytes=48 * 1024 * 1024
        ),
    )(*[
        pltpu.with_memory_space_constraint(array, pltpu.HBM)
        for array in (strain_record, jnp.asarray(fixed_tables()), dead_channels, source_channels)
    ], band_start)
    return out.reshape(2, FQ, NY * NZ * SRC, CH)


def solution(mesh):
    in_specs = (P("chan", "tm"), P(), P("chan"), P())
    out_specs = P(None, "tm", None, "chan")
    return jax.shard_map(body, mesh=mesh, in_specs=in_specs, out_specs=out_specs, check_vma=False)
```

```python
import jax
import jax.numpy as jnp
import numpy as np
from jax import lax
from jax.experimental import pallas as pl
from jax.experimental.pallas import tpu as pltpu
from jax.sharding import PartitionSpec as P

NFFT = 512
FQ = 5
NT = 16
NY, NZ = 4, 8
CH = 128
SRC = 32
HALF = 16
NCHAN = NY * NZ * CH
BLOCKS = 256
DEAD = 200
ROWS = 2 * FQ * NT
PAD = 256
EPS = 1e-06
FAR_FIRST = (4, 3, 5, 12, 11, 13, 2, 6, 10, 14, 8, 7, 9, 1, 15)
NP1, NP2 = 7, 3

UNITS = {(0, 0): (2, 0), (0, 1): (1, 0), (1, 0): (2, 1), (1, 1): (1, 1), (2, 0): (2, 2), (2, 1): (1, 2), (3, 0): (1, 3), (3, 1): (1, 4), (4, 0): (1, 5), (4, 1): (1, 6)}
PLACE = {unit: at for at, unit in UNITS.items()}
EARLY = (0, 1, 2)
GROUPS = ((0, 1), (1, 3), (3, 5))
LATE = 4
TAKE, Y1, Z1, OWN1, Z2, Y2 = range(6)
ORDER = (
    (TAKE, 0, 0), (OWN1, 0, 0), (Y1, 0, 0), (Z2, 0, 0), (TAKE, 1, 0), (OWN1, 1, 0), (Y1, 1, 0), (Z2, 1, 0),
    (OWN1, 2, 0), (Y1, 2, 0), (Z2, 2, 0), (OWN1, 0, 1), (Y1, 0, 1), (Z2, 0, 1), (OWN1, 1, 1), (TAKE, 2, 0),
    (Y1, 3, 0), (Y1, 4, 0), (Y1, 5, 0), (Y1, 6, 0), (Y1, 1, 1), (Z2, 1, 1), (OWN1, 2, 1), (Y1, 2, 1), (Z2, 2, 1),
    (OWN1, 0, 2), (Z1, 0, 0), (Z2, 0, 2), (OWN1, 1, 2), (Z2, 1, 2), (Y1, 3, 1), (OWN1, 2, 2), (Z2, 2, 2),
    (Y1, 4, 1), (OWN1, 0, 3), (Y1, 5, 1), (Z1, 0, 1), (Y1, 6, 1), (Z2, 0, 3), (OWN1, 1, 3), (Z1, 1, 0), (Z1, 2, 0),
    (Z2, 1, 3), (OWN1, 2, 3), (Z1, 3, 0), (Z2, 2, 3), (Z1, 4, 0), (Z1, 5, 0), (Z1, 6, 0), (Z1, 0, 2), (Y2, 0, 0),
    (Z1, 1, 1), (Y2, 1, 0), (Z1, 2, 1), (Z1, 3, 1), (Y2, 2, 0), (Z1, 4, 1), (Z1, 5, 1), (Y2, 0, 1), (Z1, 6, 1),
    (Z1, 0, 3), (Z1, 1, 2), (Z1, 2, 2), (Z1, 3, 2), (Y2, 1, 1), (Z1, 4, 2), (Z1, 5, 2), (Z1, 6, 2), (Z1, 0, 4),
    (Z1, 1, 3), (Y2, 2, 1), (Z1, 2, 3), (Z1, 3, 3), (Y2, 0, 2), (Z1, 4, 3), (Z1, 5, 3), (Y2, 1, 2), (Z1, 6, 3),
    (Z1, 1, 4), (Z1, 2, 4), (Z1, 3, 4), (Y2, 2, 2), (Z1, 4, 4), (Z1, 5, 4), (Z1, 6, 4),
)


def fixed_tables():
    n = np.arange(NFFT)
    taper = 0.5 - 0.5 * np.cos(2.0 * np.pi / NFFT * n)
    bins = (np.arange(FQ)[:, None] + FQ * np.arange(NT)[None, :]).reshape(-1)
    angle = 2.0 * np.pi / NFFT * (bins[:, None] * n[None, :] % NFFT)
    return np.stack([taper * np.cos(angle), taper * np.sin(angle)]).astype(np.float32)


def dot_nt(left, right):
    return lax.dot_general(left, right, (((1,), (1,)), ((), ())), preferred_element_type=jnp.float32)


def kernel(
    x_hbm, fixed_hbm, dead_hbm, source_hbm, start_ref, out_ref,
    x_ref, fixed, dead_ref, source_ref, table_ref, sel_ref, raw, sums,
    part, parts_in, line, lines_in, common, send, band, mats, g1, g2,
    in_sem, ps_send, ps_recv, re_send, re_recv, s1, r1, s2, r2,
):
    chan, tm = lax.axis_index("chan"), lax.axis_index("tm")
    y, z = lax.div(chan, NZ), lax.rem(chan, NZ)

    ys = [lax.rem(y + step, NY) for step in range(NY)]
    zs = [lax.rem(z + step, NZ) for step in range(NZ)]
    ts = [lax.rem(tm + step, NT) for step in range(NT)]
    along_y = [(ys[step] * NZ + z, tm) for step in range(NY)]
    along_z = [(y * NZ + zs[step], tm) for step in range(NZ)]

    def at_y(step):
        return along_y[step % NY]

    def at_z(step):
        return along_z[step % NZ]

    def at_t(step):
        return (chan, ts[step % NT])

    def remote(src, dst, send_sem, recv_sem, where):
        return pltpu.make_async_remote_copy(
            src_ref=src, dst_ref=dst, send_sem=send_sem, recv_sem=recv_sem,
            device_id=where, device_id_type=pl.DeviceIdType.MESH,
        )

    sent = {}

    def start(key, *args):
        copy = remote(*args)
        copy.start()
        sent.setdefault(key, []).append(copy)

    def settle(key):
        for copy in sent.pop(key, []):
            copy.wait_send()

    def arrived(ref, sem):
        pltpu.make_async_copy(ref, ref, sem).wait()

    fetches = [
        pltpu.make_async_copy(dead_hbm, dead_ref, in_sem.at[0]),
        pltpu.make_async_copy(source_hbm, source_ref, in_sem.at[1]),
        pltpu.make_async_copy(fixed_hbm, fixed, in_sem.at[2]),
    ]
    quarter = NT * NFFT // 4
    for k in range(4):
        part_of = slice(k * quarter, (k + 1) * quarter)
        fetches.append(pltpu.make_async_copy(x_hbm.at[:, part_of], x_ref.at[:, part_of], in_sem.at[3 + k]))
    for fetch in fetches:
        fetch.start()

    barrier = pltpu.get_barrier_semaphore()
    for peer in (
        [at_z(s) for s in range(1, NZ)] + [at_y(s) for s in range(1, NY)] + [at_t(s) for s in range(1, NT)]
    ):
        pl.semaphore_signal(barrier, inc=1, device_id=peer, device_id_type=pl.DeviceIdType.MESH)

    phase = start_ref[0] * lax.broadcasted_iota(jnp.int32, (8, NFFT), 1) % NFFT
    angle = 2.0 * jnp.pi / NFFT * phase.astype(jnp.float32)
    shift_cos = jnp.concatenate([jnp.cos(angle)] * 2, axis=0)
    shift_sin = jnp.concatenate([jnp.sin(angle)] * 2, axis=0)
    fetches[2].wait()
    for i in range(FQ):
        cos_i, sin_i = fixed[0, NT * i:NT * (i + 1)], fixed[1, NT * i:NT * (i + 1)]
        table_ref[32 * i:32 * i + 16] = (shift_cos * cos_i - shift_sin * sin_i).astype(jnp.bfloat16)
        table_ref[32 * i + 16:32 * i + 32] = (-(shift_sin * cos_i + shift_cos * sin_i)).astype(jnp.bfloat16)
    table_ref[ROWS:] = jnp.zeros((PAD - ROWS, NFFT), jnp.bfloat16)

    fetches[0].wait()
    ids = chan * CH + lax.broadcasted_iota(jnp.int32, (CH, DEAD), 0)
    struck = jnp.where(ids == jnp.broadcast_to(dead_ref[...][None, :], (CH, DEAD)), 1.0, 0.0)
    live_rows = jnp.broadcast_to(1.0 - jnp.max(struck, axis=1, keepdims=True), (CH, PAD))

    for k in range(4):
        fetches[3 + k].wait()
        blocks = [x_ref[:, (4 * k + b) * NFFT:(4 * k + b + 1) * NFFT] for b in range(4)]
        values = dot_nt(jnp.concatenate(blocks, axis=0), table_ref[...])
        for b in range(4):
            value = values[CH * b:CH * (b + 1)]
            sums[4 * k + b:4 * k + b + 1] = jnp.sum(value * live_rows, axis=0, keepdims=True)
    for q in range(3):
        lanes = slice(64 * q, 64 * q + 64)
        part[q] = jnp.concatenate([sums[0:8, lanes], sums[8:16, lanes]], axis=1)

    pl.semaphore_wait(barrier, (NZ - 1) + (NY - 1) + (NT - 1))

    pieces = (slice(0, 1), slice(1, 3))

    def sum_z(n):
        for s in range(1, NZ):
            start(
                "sum", part.at[pieces[n]], parts_in.at[s - 1, pieces[n]],
                ps_send.at[n, s - 1], ps_recv.at[n, s - 1], at_z(s),
            )

    def sum_y(n):
        total = part[pieces[n]]
        for s in range(1, NZ):
            arrived(parts_in.at[s - 1, pieces[n]], ps_recv.at[n, s - 1])
            total = total + parts_in[s - 1, pieces[n]]
        line[pieces[n]] = total
        for s in range(1, NY):
            start(
                "sum", line.at[pieces[n]], lines_in.at[s - 1, pieces[n]],
                ps_send.at[n, 6 + s], ps_recv.at[n, 6 + s], at_y(s),
            )

    def close_sum(n):
        total = line[pieces[n]]
        for s in range(1, NY):
            arrived(lines_in.at[s - 1, pieces[n]], ps_recv.at[n, 6 + s])
            total = total + lines_in[s - 1, pieces[n]]
        common[pieces[n]] = total / (NCHAN - DEAD)

    def transform(b, carry):
        samples = x_ref[:, pl.ds(pl.multiple_of(b * NFFT, NFFT), NFFT)]
        raw[pl.ds(b, ROWS, stride=NT), :] = dot_nt(table_ref[0:ROWS], samples)
        return carry

    sum_z(0)
    sum_z(1)
    live = live_rows[:, 0:CH].T[0:8]
    fetches[1].wait()
    source_ids = chan * CH + lax.broadcasted_iota(jnp.int32, (SRC, CH), 1)
    source_rows = lax.broadcasted_iota(jnp.int32, (SRC, CH), 0)
    wanted = jnp.zeros((SRC, CH), jnp.int32)
    for k in range(SRC):
        wanted = jnp.where(source_rows == k, source_ref[k], wanted)
    sel_ref[...] = jnp.where(wanted == source_ids, 1.0, 0.0).astype(jnp.bfloat16)
    lax.fori_loop(0, NT // 2, transform, 0)
    sum_y(0)
    sum_y(1)
    lax.fori_loop(NT // 2, NT, transform, 0)

    def give(group):
        first, last = GROUPS[group]
        for i in range(first, last):
            mode = common[i // 2]
            for p in range(2):
                for d in range(NT):
                    both = []
                    for half in range(2):
                        lane = 64 * half + 32 * (i % 2) + 16 * p + d
                        row = NT * (32 * i + 16 * p + d) + 8 * half
                        value = raw[row:row + 8]
                        both.append(live * (value - jnp.broadcast_to(mode[:, lane:lane + 1], (8, CH))))
                    send[i, d, p] = jnp.concatenate(both, axis=0).astype(jnp.bfloat16)
        for s in FAR_FIRST:
            remote(
                send.at[first:last, ts[s]], band.at[first:last, tm],
                re_send.at[group], re_recv.at[group], at_t(s),
            ).start()
        for i in range(first, last):
            band[i, tm] = send[i, tm]

    def whiten(i):
        real = band[i, :, 0].reshape(BLOCKS, CH).astype(jnp.float32)
        imag = band[i, :, 1].reshape(BLOCKS, CH).astype(jnp.float32)
        power = jnp.sum(real * real + imag * imag, axis=0, keepdims=True) / BLOCKS
        scale = lax.rsqrt(power + EPS)
        real, imag = real * scale, imag * scale
        mats[i, 0:BLOCKS, 0:CH] = real.astype(jnp.bfloat16)
        mats[i, BLOCKS:, 0:CH] = imag.astype(jnp.bfloat16)
        mats[i, 0:BLOCKS, CH:] = imag.astype(jnp.bfloat16)
        mats[i, BLOCKS:, CH:] = (-real).astype(jnp.bfloat16)
        rows = dot_nt(sel_ref[...], mats[i, :, 0:CH]).astype(jnp.bfloat16)
        for h in range(2):
            kind, u = UNITS[(i, h)]
            piece = rows[HALF * h:HALF * (h + 1)]
            if kind == 1:
                g1[u, z, 0] = piece
            else:
                g2[u, y, z] = piece

    def first_y(u, stage):
        if stage == 0:
            mine = g1.at[u, z, 0]
            start((Y1, u), mine, g1.at[u, z, 3], s1.at[u, 0], r1.at[u, 0], at_y(1))
            start((Y1, u), mine, g1.at[u, z, 1], s1.at[u, 1], r1.at[u, 1], at_y(-1))
        else:
            if u % 2 == 0:
                arrived(g1.at[u, z, 3], r1.at[u, 0])
                start((Y1, u), g1.at[u, z, 3], g1.at[u, z, 2], s1.at[u, 2], r1.at[u, 2], at_y(1))
                arrived(g1.at[u, z, 1], r1.at[u, 1])
            else:
                arrived(g1.at[u, z, 1], r1.at[u, 1])
                start((Y1, u), g1.at[u, z, 1], g1.at[u, z, 2], s1.at[u, 2], r1.at[u, 2], at_y(-1))
                arrived(g1.at[u, z, 3], r1.at[u, 0])

    def own_z(u, stage):
        left, right = zs[-stage % NZ], zs[stage]
        if stage == 4:
            arrived(g1.at[u, left, 0], r1.at[u, 17])
            return
        a, b = g1.at[u, left, 0], g1.at[u, right, 0]
        if stage > 0:
            arrived(a, r1.at[u, 9 + 2 * stage])
        if stage < 3 or u % 2 == 1:
            to = 17 if stage == 3 else 11 + 2 * stage
            start((OWN1, u), a, a, s1.at[u, to], r1.at[u, to], at_z(1))
        if stage > 0:
            arrived(b, r1.at[u, 10 + 2 * stage])
        if stage < 3 or u % 2 == 0:
            to = 17 if stage == 3 else 12 + 2 * stage
            start((OWN1, u), b, b, s1.at[u, to], r1.at[u, to], at_z(-1))

    def then_z(u, stage):
        low = 1 if u in EARLY else 0
        middle = 2 if low == 0 or u % 2 == 1 else 3
        left, right = zs[-stage % NZ], zs[stage]
        if stage == 4:
            arrived(g1.at[u, left, low:middle], r1.at[u, 9])
            arrived(g1.at[u, left, middle:4], r1.at[u, 10])
            if low:
                own_z(u, 4)
            lines(u, (4,))
            return
        if stage < 3:
            a, b = g1.at[u, left, low:4], g1.at[u, right, low:4]
        else:
            a, b = g1.at[u, left, low:middle], g1.at[u, right, middle:4]
        if stage == 0:
            arrived(g1.at[u, z, 2], r1.at[u, 2])
        else:
            arrived(g1.at[u, left, low:4], r1.at[u, 1 + 2 * stage])
        start((Z1, u, stage == 3), a, a, s1.at[u, 3 + 2 * stage], r1.at[u, 3 + 2 * stage], at_z(1))
        if stage > 0:
            arrived(g1.at[u, right, low:4], r1.at[u, 2 + 2 * stage])
        start((Z1, u, stage == 3), b, b, s1.at[u, 4 + 2 * stage], r1.at[u, 4 + 2 * stage], at_z(-1))
        if stage == 3:
            for steps in ((-3, -2, -1, 0), (1, 2, 3)):
                lines(u, steps)
            for key in ((Y1, u), (OWN1, u), (Z1, u, False)):
                settle(key)

    def lines(u, steps):
        i, h = PLACE[(1, u)]
        at = [zs[step % NZ] for step in steps]
        left = jnp.concatenate([g1[u, zz].reshape(NY * HALF, 2 * BLOCKS) for zz in at], axis=0)
        both = jnp.dot(left, mats[i], preferred_element_type=jnp.float32) * (1.0 / BLOCKS)
        both = both.astype(jnp.bfloat16).reshape(len(steps), NY, HALF, 2 * CH)
        for k, zz in enumerate(at):
            for up in range(NY):
                out_ref[0, i, ys[up], zz, h] = both[k, up, :, 0:CH]
                out_ref[1, i, ys[up], zz, h] = both[k, up, :, CH:]

    def first_z(u, stage):
        left, right = zs[-stage % NZ], zs[stage]
        a, b = g2.at[u, y, left], g2.at[u, y, right]
        if stage > 0:
            arrived(a, r2.at[u, 2 * stage - 2])
        if stage < 3 or u % 2 == 0:
            start((Z2, u), a, a, s2.at[u, 2 * stage], r2.at[u, 2 * stage], at_z(1))
        if stage > 0:
            arrived(b, r2.at[u, 2 * stage - 1])
        if stage < 3 or u % 2 == 1:
            start((Z2, u), b, b, s2.at[u, 2 * stage + 1], r2.at[u, 2 * stage + 1], at_z(-1))

    def then_y(u, stage):
        down, up, far = ys[3], ys[1], ys[2]
        if stage == 0:
            arrived(g2.at[u, y, zs[4]], r2.at[u, 6 + u % 2])
            start((Y2, u, 0), g2.at[u, y], g2.at[u, y], s2.at[u, 8], r2.at[u, 8], at_y(1))
            start((Y2, u, 0), g2.at[u, y], g2.at[u, y], s2.at[u, 9], r2.at[u, 9], at_y(-1))
        elif stage == 1:
            a, b = g2.at[u, down, 0:4], g2.at[u, up, 4:8]
            arrived(g2.at[u, down], r2.at[u, 8])
            start((Y2, u, 1), a, a, s2.at[u, 10], r2.at[u, 10], at_y(1))
            arrived(g2.at[u, up], r2.at[u, 9])
            start((Y2, u, 1), b, b, s2.at[u, 11], r2.at[u, 11], at_y(-1))
            columns(u, (-1, 0, 1))
            settle((Z2, u))
        else:
            arrived(g2.at[u, far, 0:4], r2.at[u, 10])
            arrived(g2.at[u, far, 4:8], r2.at[u, 11])
            columns(u, (2,))
            settle((Y2, u, 0))

    def columns(u, steps):
        i, h = PLACE[(2, u)]
        at = [ys[step % NY] for step in steps]
        left = jnp.concatenate([g2[u, yy].reshape(NZ * HALF, 2 * BLOCKS) for yy in at], axis=0)
        both = jnp.dot(left, mats[i], preferred_element_type=jnp.float32) * (1.0 / BLOCKS)
        both = both.astype(jnp.bfloat16).reshape(len(steps), NZ, HALF, 2 * CH)
        for k, yy in enumerate(at):
            out_ref[0, i, yy, :, h] = both[k, :, :, 0:CH]
            out_ref[1, i, yy, :, h] = both[k, :, :, CH:]

    def take(group):
        first, last = GROUPS[group]
        arrived(band.at[first:last, 0:NT - 1], re_recv.at[group])
        for i in range(first, last):
            whiten(i)

    def free(group):
        first, last = GROUPS[group]
        arrived(send.at[first:last, 0:NT - 1], re_send.at[group])

    steps = (take, first_y, then_z, own_z, first_z, then_y)
    close_sum(0)
    give(0)
    close_sum(1)
    give(1)
    for at, (step, unit, stage) in enumerate(ORDER):
        if at == LATE:
            give(2)
        if at == LATE + 44:
            settle("sum")
            for group in range(len(GROUPS)):
                free(group)
        if step == TAKE:
            take(unit)
        else:
            steps[step](unit, stage)
    for key in list(sent):
        settle(key)


def body(strain_record, dead_channels, source_channels, band_start):
    vmem = pl.BlockSpec(memory_space=pltpu.VMEM)
    hbm = pl.BlockSpec(memory_space=pltpu.HBM)
    dma = pltpu.SemaphoreType.DMA
    out = pl.pallas_call(
        kernel,
        out_shape=jax.ShapeDtypeStruct((2, FQ, NY, NZ, 2, HALF, CH), jnp.bfloat16),
        in_specs=[hbm] * 4 + [pl.BlockSpec(memory_space=pltpu.SMEM)],
        out_specs=vmem,
        scratch_shapes=[
            pltpu.VMEM((CH, NT * NFFT), jnp.bfloat16),
            pltpu.VMEM((2, FQ * NT, NFFT), jnp.float32),
            pltpu.VMEM((DEAD,), jnp.int32),
            pltpu.SMEM((SRC,), jnp.int32),
            pltpu.VMEM((PAD, NFFT), jnp.bfloat16),
            pltpu.VMEM((SRC, CH), jnp.bfloat16),
            pltpu.VMEM((NT * ROWS, CH), jnp.float32),
            pltpu.VMEM((NT, PAD), jnp.float32),
            pltpu.VMEM((3, 8, CH), jnp.float32),
            pltpu.VMEM((NZ - 1, 3, 8, CH), jnp.float32),
            pltpu.VMEM((3, 8, CH), jnp.float32),
            pltpu.VMEM((NY - 1, 3, 8, CH), jnp.float32),
            pltpu.VMEM((3, 8, CH), jnp.float32),
            pltpu.VMEM((FQ, NT, 2, NT, CH), jnp.bfloat16),
            pltpu.VMEM((FQ, NT, 2, NT, CH), jnp.bfloat16),
            pltpu.VMEM((FQ, 2 * BLOCKS, 2 * CH), jnp.bfloat16),
            pltpu.VMEM((NP1, NZ, NY, HALF, 2 * BLOCKS), jnp.bfloat16),
            pltpu.VMEM((NP2, NY, NZ, HALF, 2 * BLOCKS), jnp.bfloat16),
            dma((7,)), dma((2, 10)), dma((2, 10)), dma((3,)), dma((3,)),
            dma((NP1, 18)), dma((NP1, 18)), dma((NP2, 12)), dma((NP2, 12)),
        ],
        compiler_params=pltpu.CompilerParams(
            collective_id=0, has_side_effects=True, vmem_limit_bytes=48 * 1024 * 1024
        ),
    )(*[
        pltpu.with_memory_space_constraint(array, pltpu.HBM)
        for array in (strain_record, jnp.asarray(fixed_tables()), dead_channels, source_channels)
    ], band_start)
    return out.reshape(2, FQ, NY * NZ * SRC, CH)


def solution(mesh):
    in_specs = (P("chan", "tm"), P(), P("chan"), P())
    out_specs = P(None, "tm", None, "chan")
    return jax.shard_map(body, mesh=mesh, in_specs=in_specs, out_specs=out_specs, check_vma=False)
```

```python
import jax
import jax.numpy as jnp
import numpy as np
from jax import lax
from jax.experimental import pallas as pl
from jax.experimental.pallas import tpu as pltpu
from jax.sharding import PartitionSpec as P

NFFT = 512
FQ = 5
NT = 16
NY, NZ = 4, 8
CH = 128
SRC = 32
HALF = 16
NCHAN = NY * NZ * CH
BLOCKS = 256
DEAD = 200
ROWS = 2 * FQ * NT
PAD = 256
EPS = 1e-06
FAR_FIRST = (4, 3, 5, 12, 11, 13, 2, 6, 10, 14, 8, 7, 9, 1, 15)
NP1, NP2 = 7, 3

UNITS = {(0, 0): (2, 0), (0, 1): (1, 0), (1, 0): (2, 1), (1, 1): (1, 1), (2, 0): (2, 2), (2, 1): (1, 2), (3, 0): (1, 3), (3, 1): (1, 4), (4, 0): (1, 5), (4, 1): (1, 6)}
PLACE = {unit: at for at, unit in UNITS.items()}
EARLY = (0, 1, 2)
GROUPS = ((0, 1), (1, 3), (3, 5))
LATE = 4
TAKE, Y1, Z1, OWN1, Z2, Y2 = range(6)
ORDER = (
    (TAKE, 0, 0), (OWN1, 0, 0), (Y1, 0, 0), (Z2, 0, 0), (TAKE, 1, 0), (OWN1, 1, 0), (Y1, 1, 0), (Z2, 1, 0),
    (OWN1, 2, 0), (Y1, 2, 0), (Z2, 2, 0), (OWN1, 0, 1), (Y1, 0, 1), (Z2, 0, 1), (OWN1, 1, 1), (TAKE, 2, 0),
    (Y1, 3, 0), (Y1, 4, 0), (Y1, 5, 0), (Y1, 6, 0), (Y1, 1, 1), (Z2, 1, 1), (OWN1, 2, 1), (Y1, 2, 1), (Z2, 2, 1),
    (OWN1, 0, 2), (Z1, 0, 0), (Z2, 0, 2), (OWN1, 1, 2), (Z2, 1, 2), (Y1, 3, 1), (OWN1, 2, 2), (Z2, 2, 2),
    (Y1, 4, 1), (OWN1, 0, 3), (Y1, 5, 1), (Z1, 0, 1), (Y1, 6, 1), (Z2, 0, 3), (OWN1, 1, 3), (Z1, 1, 0), (Z1, 2, 0),
    (Z2, 1, 3), (OWN1, 2, 3), (Z1, 3, 0), (Z2, 2, 3), (Z1, 4, 0), (Z1, 5, 0), (Z1, 6, 0), (Z1, 0, 2), (Y2, 0, 0),
    (Z1, 1, 1), (Y2, 1, 0), (Z1, 2, 1), (Z1, 3, 1), (Y2, 2, 0), (Z1, 4, 1), (Z1, 5, 1), (Y2, 0, 1), (Z1, 6, 1),
    (Z1, 0, 3), (Z1, 1, 2), (Z1, 2, 2), (Z1, 3, 2), (Y2, 1, 1), (Z1, 4, 2), (Z1, 5, 2), (Z1, 6, 2), (Z1, 0, 4),
    (Z1, 1, 3), (Y2, 2, 1), (Z1, 2, 3), (Z1, 3, 3), (Y2, 0, 2), (Z1, 4, 3), (Z1, 5, 3), (Y2, 1, 2), (Z1, 6, 3),
    (Z1, 1, 4), (Z1, 2, 4), (Z1, 3, 4), (Y2, 2, 2), (Z1, 4, 4), (Z1, 5, 4), (Z1, 6, 4),
)


def fixed_tables():
    n = np.arange(NFFT)
    taper = 0.5 - 0.5 * np.cos(2.0 * np.pi / NFFT * n)
    bins = (np.arange(FQ)[:, None] + FQ * np.arange(NT)[None, :]).reshape(-1)
    angle = 2.0 * np.pi / NFFT * (bins[:, None] * n[None, :] % NFFT)
    return np.stack([taper * np.cos(angle), taper * np.sin(angle)]).astype(np.float32)


def dot_nt(left, right):
    return lax.dot_general(left, right, (((1,), (1,)), ((), ())), preferred_element_type=jnp.float32)


def kernel(
    x_hbm, fixed_hbm, dead_hbm, source_hbm, start_ref, out_ref,
    x_ref, fixed, dead_ref, source_ref, table_ref, sel_ref, raw, sums,
    part, parts_in, line, lines_in, common, send, band, mats, g1, g2,
    in_sem, ps_send, ps_recv, re_send, re_recv, s1, r1, s2, r2,
):
    chan, tm = lax.axis_index("chan"), lax.axis_index("tm")
    y, z = lax.div(chan, NZ), lax.rem(chan, NZ)

    ys = [lax.rem(y + step, NY) for step in range(NY)]
    zs = [lax.rem(z + step, NZ) for step in range(NZ)]
    ts = [lax.rem(tm + step, NT) for step in range(NT)]
    along_y = [(ys[step] * NZ + z, tm) for step in range(NY)]
    along_z = [(y * NZ + zs[step], tm) for step in range(NZ)]

    def at_y(step):
        return along_y[step % NY]

    def at_z(step):
        return along_z[step % NZ]

    def at_t(step):
        return (chan, ts[step % NT])

    def remote(src, dst, send_sem, recv_sem, where):
        return pltpu.make_async_remote_copy(
            src_ref=src, dst_ref=dst, send_sem=send_sem, recv_sem=recv_sem,
            device_id=where, device_id_type=pl.DeviceIdType.MESH,
        )

    sent = {}

    def start(key, *args):
        copy = remote(*args)
        copy.start()
        sent.setdefault(key, []).append(copy)

    def settle(key):
        for copy in sent.pop(key, []):
            copy.wait_send()

    def arrived(ref, sem):
        pltpu.make_async_copy(ref, ref, sem).wait()

    fetches = [
        pltpu.make_async_copy(dead_hbm, dead_ref, in_sem.at[0]),
        pltpu.make_async_copy(source_hbm, source_ref, in_sem.at[1]),
        pltpu.make_async_copy(fixed_hbm, fixed, in_sem.at[2]),
    ]
    quarter = NT * NFFT // 4
    for k in range(4):
        part_of = slice(k * quarter, (k + 1) * quarter)
        fetches.append(pltpu.make_async_copy(x_hbm.at[:, part_of], x_ref.at[:, part_of], in_sem.at[3 + k]))
    for fetch in fetches:
        fetch.start()

    barrier = pltpu.get_barrier_semaphore()
    for peer in (
        [at_z(s) for s in range(1, NZ)] + [at_y(s) for s in range(1, NY)] + [at_t(s) for s in range(1, NT)]
    ):
        pl.semaphore_signal(barrier, inc=1, device_id=peer, device_id_type=pl.DeviceIdType.MESH)

    phase = start_ref[0] * lax.broadcasted_iota(jnp.int32, (8, NFFT), 1) % NFFT
    angle = 2.0 * jnp.pi / NFFT * phase.astype(jnp.float32)
    shift_cos = jnp.concatenate([jnp.cos(angle)] * 2, axis=0)
    shift_sin = jnp.concatenate([jnp.sin(angle)] * 2, axis=0)
    fetches[2].wait()
    for i in range(FQ):
        cos_i, sin_i = fixed[0, NT * i:NT * (i + 1)], fixed[1, NT * i:NT * (i + 1)]
        table_ref[32 * i:32 * i + 16] = (shift_cos * cos_i - shift_sin * sin_i).astype(jnp.bfloat16)
        table_ref[32 * i + 16:32 * i + 32] = (-(shift_sin * cos_i + shift_cos * sin_i)).astype(jnp.bfloat16)
    table_ref[ROWS:] = jnp.zeros((PAD - ROWS, NFFT), jnp.bfloat16)

    fetches[0].wait()
    ids = chan * CH + lax.broadcasted_iota(jnp.int32, (CH, DEAD), 0)
    struck = jnp.where(ids == jnp.broadcast_to(dead_ref[...][None, :], (CH, DEAD)), 1.0, 0.0)
    live_rows = jnp.broadcast_to(1.0 - jnp.max(struck, axis=1, keepdims=True), (CH, PAD))

    for k in range(4):
        fetches[3 + k].wait()
        blocks = [x_ref[:, (4 * k + b) * NFFT:(4 * k + b + 1) * NFFT] for b in range(4)]
        values = dot_nt(jnp.concatenate(blocks, axis=0), table_ref[...])
        for b in range(4):
            value = values[CH * b:CH * (b + 1)]
            sums[4 * k + b:4 * k + b + 1] = jnp.sum(value * live_rows, axis=0, keepdims=True)
    for q in range(3):
        lanes = slice(64 * q, 64 * q + 64)
        part[q] = jnp.concatenate([sums[0:8, lanes], sums[8:16, lanes]], axis=1)

    pl.semaphore_wait(barrier, (NZ - 1) + (NY - 1) + (NT - 1))

    pieces = (slice(0, 1), slice(1, 3))

    def sum_z(n):
        for s in range(1, NZ):
            start(
                "sum", part.at[pieces[n]], parts_in.at[s - 1, pieces[n]],
                ps_send.at[n, s - 1], ps_recv.at[n, s - 1], at_z(s),
            )

    def sum_y(n):
        total = part[pieces[n]]
        for s in range(1, NZ):
            arrived(parts_in.at[s - 1, pieces[n]], ps_recv.at[n, s - 1])
            total = total + parts_in[s - 1, pieces[n]]
        line[pieces[n]] = total
        for s in range(1, NY):
            start(
                "sum", line.at[pieces[n]], lines_in.at[s - 1, pieces[n]],
                ps_send.at[n, 6 + s], ps_recv.at[n, 6 + s], at_y(s),
            )

    def close_sum(n):
        total = line[pieces[n]]
        for s in range(1, NY):
            arrived(lines_in.at[s - 1, pieces[n]], ps_recv.at[n, 6 + s])
            total = total + lines_in[s - 1, pieces[n]]
        common[pieces[n]] = total / (NCHAN - DEAD)

    def transform(b, carry):
        samples = x_ref[:, pl.ds(pl.multiple_of(b * NFFT, NFFT), NFFT)]
        raw[pl.ds(b, ROWS, stride=NT), :] = dot_nt(table_ref[0:ROWS], samples)
        return carry

    sum_z(0)
    sum_z(1)
    live = live_rows[:, 0:CH].T[0:8]
    fetches[1].wait()
    source_ids = chan * CH + lax.broadcasted_iota(jnp.int32, (SRC, CH), 1)
    source_rows = lax.broadcasted_iota(jnp.int32, (SRC, CH), 0)
    wanted = jnp.zeros((SRC, CH), jnp.int32)
    for k in range(SRC):
        wanted = jnp.where(source_rows == k, source_ref[k], wanted)
    sel_ref[...] = jnp.where(wanted == source_ids, 1.0, 0.0).astype(jnp.bfloat16)
    lax.fori_loop(0, 8, transform, 0, unroll=4)
    sum_y(0)
    lax.fori_loop(8, 12, transform, 0, unroll=4)
    sum_y(1)
    lax.fori_loop(12, NT, transform, 0, unroll=4)

    def give(group):
        first, last = GROUPS[group]
        for i in range(first, last):
            mode = common[i // 2]
            for p in range(2):
                for d in range(NT):
                    both = []
                    for half in range(2):
                        lane = 64 * half + 32 * (i % 2) + 16 * p + d
                        row = NT * (32 * i + 16 * p + d) + 8 * half
                        value = raw[row:row + 8]
                        both.append(live * (value - jnp.broadcast_to(mode[:, lane:lane + 1], (8, CH))))
                    send[i, d, p] = jnp.concatenate(both, axis=0).astype(jnp.bfloat16)
        for s in FAR_FIRST:
            remote(
                send.at[first:last, ts[s]], band.at[first:last, tm],
                re_send.at[group], re_recv.at[group], at_t(s),
            ).start()
        for i in range(first, last):
            band[i, tm] = send[i, tm]

    def whiten(i):
        real = band[i, :, 0].reshape(BLOCKS, CH).astype(jnp.float32)
        imag = band[i, :, 1].reshape(BLOCKS, CH).astype(jnp.float32)
        power = jnp.sum(real * real + imag * imag, axis=0, keepdims=True) / BLOCKS
        scale = lax.rsqrt(power + EPS)
        real, imag = real * scale, imag * scale
        mats[i, 0:BLOCKS, 0:CH] = real.astype(jnp.bfloat16)
        mats[i, BLOCKS:, 0:CH] = imag.astype(jnp.bfloat16)
        mats[i, 0:BLOCKS, CH:] = imag.astype(jnp.bfloat16)
        mats[i, BLOCKS:, CH:] = (-real).astype(jnp.bfloat16)
        rows = dot_nt(sel_ref[...], mats[i, :, 0:CH]).astype(jnp.bfloat16)
        for h in range(2):
            kind, u = UNITS[(i, h)]
            piece = rows[HALF * h:HALF * (h + 1)]
            if kind == 1:
                g1[u, z, 0] = piece
            else:
                g2[u, y, z] = piece

    def first_y(u, stage):
        if stage == 0:
            mine = g1.at[u, z, 0]
            start((Y1, u), mine, g1.at[u, z, 3], s1.at[u, 0], r1.at[u, 0], at_y(1))
            start((Y1, u), mine, g1.at[u, z, 1], s1.at[u, 1], r1.at[u, 1], at_y(-1))
        else:
            if u % 2 == 0:
                arrived(g1.at[u, z, 3], r1.at[u, 0])
                start((Y1, u), g1.at[u, z, 3], g1.at[u, z, 2], s1.at[u, 2], r1.at[u, 2], at_y(1))
                arrived(g1.at[u, z, 1], r1.at[u, 1])
            else:
                arrived(g1.at[u, z, 1], r1.at[u, 1])
                start((Y1, u), g1.at[u, z, 1], g1.at[u, z, 2], s1.at[u, 2], r1.at[u, 2], at_y(-1))
                arrived(g1.at[u, z, 3], r1.at[u, 0])

    def own_z(u, stage):
        left, right = zs[-stage % NZ], zs[stage]
        if stage == 4:
            arrived(g1.at[u, left, 0], r1.at[u, 17])
            return
        a, b = g1.at[u, left, 0], g1.at[u, right, 0]
        if stage > 0:
            arrived(a, r1.at[u, 9 + 2 * stage])
        if stage < 3 or u % 2 == 1:
            to = 17 if stage == 3 else 11 + 2 * stage
            start((OWN1, u), a, a, s1.at[u, to], r1.at[u, to], at_z(1))
        if stage > 0:
            arrived(b, r1.at[u, 10 + 2 * stage])
        if stage < 3 or u % 2 == 0:
            to = 17 if stage == 3 else 12 + 2 * stage
            start((OWN1, u), b, b, s1.at[u, to], r1.at[u, to], at_z(-1))

    def then_z(u, stage):
        low = 1 if u in EARLY else 0
        middle = 2 if low == 0 or u % 2 == 1 else 3
        left, right = zs[-stage % NZ], zs[stage]
        if stage == 4:
            arrived(g1.at[u, left, low:middle], r1.at[u, 9])
            arrived(g1.at[u, left, middle:4], r1.at[u, 10])
            if low:
                own_z(u, 4)
            lines(u, (4,))
            return
        if stage < 3:
            a, b = g1.at[u, left, low:4], g1.at[u, right, low:4]
        else:
            a, b = g1.at[u, left, low:middle], g1.at[u, right, middle:4]
        if stage == 0:
            arrived(g1.at[u, z, 2], r1.at[u, 2])
        else:
            arrived(g1.at[u, left, low:4], r1.at[u, 1 + 2 * stage])
        start((Z1, u, stage == 3), a, a, s1.at[u, 3 + 2 * stage], r1.at[u, 3 + 2 * stage], at_z(1))
        if stage > 0:
            arrived(g1.at[u, right, low:4], r1.at[u, 2 + 2 * stage])
        start((Z1, u, stage == 3), b, b, s1.at[u, 4 + 2 * stage], r1.at[u, 4 + 2 * stage], at_z(-1))
        if stage == 3:
            lines(u, (-3, -2, -1, 0, 1, 2, 3))
            for key in ((Y1, u), (OWN1, u), (Z1, u, False)):
                settle(key)

    def lines(u, steps):
        i, h = PLACE[(1, u)]
        at = [zs[step % NZ] for step in steps]
        left = jnp.concatenate([g1[u, zz].reshape(NY * HALF, 2 * BLOCKS) for zz in at], axis=0)
        both = jnp.dot(left, mats[i], preferred_element_type=jnp.float32) * (1.0 / BLOCKS)
        both = both.astype(jnp.bfloat16).reshape(len(steps), NY, HALF, 2 * CH)
        for k, zz in enumerate(at):
            for up in range(NY):
                out_ref[0, i, ys[up], zz, h] = both[k, up, :, 0:CH]
                out_ref[1, i, ys[up], zz, h] = both[k, up, :, CH:]

    def first_z(u, stage):
        left, right = zs[-stage % NZ], zs[stage]
        a, b = g2.at[u, y, left], g2.at[u, y, right]
        if stage > 0:
            arrived(a, r2.at[u, 2 * stage - 2])
        if stage < 3 or u % 2 == 0:
            start((Z2, u), a, a, s2.at[u, 2 * stage], r2.at[u, 2 * stage], at_z(1))
        if stage > 0:
            arrived(b, r2.at[u, 2 * stage - 1])
        if stage < 3 or u % 2 == 1:
            start((Z2, u), b, b, s2.at[u, 2 * stage + 1], r2.at[u, 2 * stage + 1], at_z(-1))

    def then_y(u, stage):
        down, up, far = ys[3], ys[1], ys[2]
        if stage == 0:
            arrived(g2.at[u, y, zs[4]], r2.at[u, 6 + u % 2])
            start((Y2, u, 0), g2.at[u, y], g2.at[u, y], s2.at[u, 8], r2.at[u, 8], at_y(1))
            start((Y2, u, 0), g2.at[u, y], g2.at[u, y], s2.at[u, 9], r2.at[u, 9], at_y(-1))
        elif stage == 1:
            a, b = g2.at[u, down, 0:4], g2.at[u, up, 4:8]
            arrived(g2.at[u, down], r2.at[u, 8])
            start((Y2, u, 1), a, a, s2.at[u, 10], r2.at[u, 10], at_y(1))
            arrived(g2.at[u, up], r2.at[u, 9])
            start((Y2, u, 1), b, b, s2.at[u, 11], r2.at[u, 11], at_y(-1))
            columns(u, (-1, 0, 1))
            settle((Z2, u))
        else:
            arrived(g2.at[u, far, 0:4], r2.at[u, 10])
            arrived(g2.at[u, far, 4:8], r2.at[u, 11])
            columns(u, (2,))
            settle((Y2, u, 0))

    def columns(u, steps):
        i, h = PLACE[(2, u)]
        at = [ys[step % NY] for step in steps]
        left = jnp.concatenate([g2[u, yy].reshape(NZ * HALF, 2 * BLOCKS) for yy in at], axis=0)
        both = jnp.dot(left, mats[i], preferred_element_type=jnp.float32) * (1.0 / BLOCKS)
        both = both.astype(jnp.bfloat16).reshape(len(steps), NZ, HALF, 2 * CH)
        for k, yy in enumerate(at):
            out_ref[0, i, yy, :, h] = both[k, :, :, 0:CH]
            out_ref[1, i, yy, :, h] = both[k, :, :, CH:]

    def take(group):
        first, last = GROUPS[group]
        arrived(band.at[first:last, 0:NT - 1], re_recv.at[group])
        for i in range(first, last):
            whiten(i)

    def free(group):
        first, last = GROUPS[group]
        arrived(send.at[first:last, 0:NT - 1], re_send.at[group])

    steps = (take, first_y, then_z, own_z, first_z, then_y)
    close_sum(0)
    give(0)
    close_sum(1)
    give(1)
    for at, (step, unit, stage) in enumerate(ORDER):
        if at == LATE:
            give(2)
        if at == LATE + 44:
            settle("sum")
            for group in range(len(GROUPS)):
                free(group)
        if step == TAKE:
            take(unit)
        else:
            steps[step](unit, stage)
    for key in list(sent):
        settle(key)


def body(strain_record, dead_channels, source_channels, band_start):
    vmem = pl.BlockSpec(memory_space=pltpu.VMEM)
    hbm = pl.BlockSpec(memory_space=pltpu.HBM)
    dma = pltpu.SemaphoreType.DMA
    out = pl.pallas_call(
        kernel,
        out_shape=jax.ShapeDtypeStruct((2, FQ, NY, NZ, 2, HALF, CH), jnp.bfloat16),
        in_specs=[hbm] * 4 + [pl.BlockSpec(memory_space=pltpu.SMEM)],
        out_specs=vmem,
        scratch_shapes=[
            pltpu.VMEM((CH, NT * NFFT), jnp.bfloat16),
            pltpu.VMEM((2, FQ * NT, NFFT), jnp.float32),
            pltpu.VMEM((DEAD,), jnp.int32),
            pltpu.SMEM((SRC,), jnp.int32),
            pltpu.VMEM((PAD, NFFT), jnp.bfloat16),
            pltpu.VMEM((SRC, CH), jnp.bfloat16),
            pltpu.VMEM((NT * ROWS, CH), jnp.float32),
            pltpu.VMEM((NT, PAD), jnp.float32),
            pltpu.VMEM((3, 8, CH), jnp.float32),
            pltpu.VMEM((NZ - 1, 3, 8, CH), jnp.float32),
            pltpu.VMEM((3, 8, CH), jnp.float32),
            pltpu.VMEM((NY - 1, 3, 8, CH), jnp.float32),
            pltpu.VMEM((3, 8, CH), jnp.float32),
            pltpu.VMEM((FQ, NT, 2, NT, CH), jnp.bfloat16),
            pltpu.VMEM((FQ, NT, 2, NT, CH), jnp.bfloat16),
            pltpu.VMEM((FQ, 2 * BLOCKS, 2 * CH), jnp.bfloat16),
            pltpu.VMEM((NP1, NZ, NY, HALF, 2 * BLOCKS), jnp.bfloat16),
            pltpu.VMEM((NP2, NY, NZ, HALF, 2 * BLOCKS), jnp.bfloat16),
            dma((7,)), dma((2, 10)), dma((2, 10)), dma((3,)), dma((3,)),
            dma((NP1, 18)), dma((NP1, 18)), dma((NP2, 12)), dma((NP2, 12)),
        ],
        compiler_params=pltpu.CompilerParams(
            collective_id=0, has_side_effects=True, vmem_limit_bytes=48 * 1024 * 1024
        ),
    )(*[
        pltpu.with_memory_space_constraint(array, pltpu.HBM)
        for array in (strain_record, jnp.asarray(fixed_tables()), dead_channels, source_channels)
    ], band_start)
    return out.reshape(2, FQ, NY * NZ * SRC, CH)


def solution(mesh):
    in_specs = (P("chan", "tm"), P(), P("chan"), P())
    out_specs = P(None, "tm", None, "chan")
    return jax.shard_map(body, mesh=mesh, in_specs=in_specs, out_specs=out_specs, check_vma=False)
```

```python
import jax
import jax.numpy as jnp
import numpy as np
from jax import lax
from jax.experimental import pallas as pl
from jax.experimental.pallas import tpu as pltpu
from jax.sharding import PartitionSpec as P

NFFT = 512
FQ = 5
NT = 16
NY, NZ = 4, 8
CH = 128
SRC = 32
HALF = 16
NCHAN = NY * NZ * CH
BLOCKS = 256
DEAD = 200
ROWS = 2 * FQ * NT
PAD = 256
EPS = 1e-06
FAR_FIRST = (4, 3, 5, 12, 11, 13, 2, 6, 10, 14, 8, 7, 9, 1, 15)
NP1, NP2 = 7, 3

UNITS = {(0, 0): (2, 0), (0, 1): (1, 0), (1, 0): (2, 1), (1, 1): (1, 1), (2, 0): (2, 2), (2, 1): (1, 2), (3, 0): (1, 3), (3, 1): (1, 4), (4, 0): (1, 5), (4, 1): (1, 6)}
PLACE = {unit: at for at, unit in UNITS.items()}
EARLY = (0, 1, 2)
GROUPS = ((0, 1), (1, 3), (3, 5))
LATE = 4
TAKE, Y1, Z1, OWN1, Z2, Y2 = range(6)
ORDER = (
    (TAKE, 0, 0), (OWN1, 0, 0), (Y1, 0, 0), (Z2, 0, 0), (TAKE, 1, 0), (OWN1, 1, 0), (Y1, 1, 0), (Z2, 1, 0),
    (OWN1, 2, 0), (Y1, 2, 0), (Z2, 2, 0), (OWN1, 0, 1), (Y1, 0, 1), (Z2, 0, 1), (OWN1, 1, 1), (TAKE, 2, 0),
    (Y1, 3, 0), (Y1, 4, 0), (Y1, 5, 0), (Y1, 6, 0), (Y1, 1, 1), (Z2, 1, 1), (OWN1, 2, 1), (Y1, 2, 1), (Z2, 2, 1),
    (OWN1, 0, 2), (Z1, 0, 0), (Z2, 0, 2), (OWN1, 1, 2), (Z2, 1, 2), (Y1, 3, 1), (OWN1, 2, 2), (Z2, 2, 2),
    (Y1, 4, 1), (OWN1, 0, 3), (Y1, 5, 1), (Z1, 0, 1), (Y1, 6, 1), (Z2, 0, 3), (OWN1, 1, 3), (Z1, 1, 0), (Z1, 2, 0),
    (Z2, 1, 3), (OWN1, 2, 3), (Z1, 3, 0), (Z2, 2, 3), (Z1, 4, 0), (Z1, 5, 0), (Z1, 6, 0), (Z1, 0, 2), (Y2, 0, 0),
    (Z1, 1, 1), (Y2, 1, 0), (Z1, 2, 1), (Z1, 3, 1), (Y2, 2, 0), (Z1, 4, 1), (Z1, 5, 1), (Z1, 6, 1), (Z1, 0, 3),
    (Z1, 1, 2), (Z1, 2, 2), (Z1, 3, 2), (Z1, 4, 2), (Z1, 5, 2), (Z1, 6, 2), (Y2, 0, 1), (Z1, 0, 4), (Z1, 1, 3),
    (Y2, 1, 1), (Z1, 2, 3), (Y2, 2, 1), (Z1, 3, 3), (Z1, 4, 3), (Z1, 5, 3), (Z1, 6, 3), (Z1, 1, 4), (Z1, 2, 4),
    (Z1, 3, 4), (Z1, 4, 4), (Z1, 5, 4), (Z1, 6, 4), (Y2, 0, 2), (Y2, 1, 2), (Y2, 2, 2),
)


def fixed_tables():
    n = np.arange(NFFT)
    taper = 0.5 - 0.5 * np.cos(2.0 * np.pi / NFFT * n)
    bins = (np.arange(FQ)[:, None] + FQ * np.arange(NT)[None, :]).reshape(-1)
    angle = 2.0 * np.pi / NFFT * (bins[:, None] * n[None, :] % NFFT)
    return np.stack([taper * np.cos(angle), taper * np.sin(angle)]).astype(np.float32)


def dot_nt(left, right):
    return lax.dot_general(left, right, (((1,), (1,)), ((), ())), preferred_element_type=jnp.float32)


def kernel(
    x_hbm, fixed_hbm, dead_hbm, source_hbm, start_ref, out_ref,
    x_ref, fixed, dead_ref, source_ref, table_ref, sel_ref, raw, sums,
    part, parts_in, line, lines_in, common, send, band, mats, g1, g2,
    in_sem, ps_send, ps_recv, re_send, re_recv, s1, r1, s2, r2,
):
    chan, tm = lax.axis_index("chan"), lax.axis_index("tm")
    y, z = lax.div(chan, NZ), lax.rem(chan, NZ)

    ys = [lax.rem(y + step, NY) for step in range(NY)]
    zs = [lax.rem(z + step, NZ) for step in range(NZ)]
    ts = [lax.rem(tm + step, NT) for step in range(NT)]
    along_y = [(ys[step] * NZ + z, tm) for step in range(NY)]
    along_z = [(y * NZ + zs[step], tm) for step in range(NZ)]

    def at_y(step):
        return along_y[step % NY]

    def at_z(step):
        return along_z[step % NZ]

    def at_t(step):
        return (chan, ts[step % NT])

    def remote(src, dst, send_sem, recv_sem, where):
        return pltpu.make_async_remote_copy(
            src_ref=src, dst_ref=dst, send_sem=send_sem, recv_sem=recv_sem,
            device_id=where, device_id_type=pl.DeviceIdType.MESH,
        )

    sent = {}

    def start(key, *args):
        copy = remote(*args)
        copy.start()
        sent.setdefault(key, []).append(copy)

    def settle(key):
        for copy in sent.pop(key, []):
            copy.wait_send()

    def arrived(ref, sem):
        pltpu.make_async_copy(ref, ref, sem).wait()

    fetches = [
        pltpu.make_async_copy(dead_hbm, dead_ref, in_sem.at[0]),
        pltpu.make_async_copy(source_hbm, source_ref, in_sem.at[1]),
        pltpu.make_async_copy(fixed_hbm, fixed, in_sem.at[2]),
    ]
    quarter = NT * NFFT // 4
    for k in range(4):
        part_of = slice(k * quarter, (k + 1) * quarter)
        fetches.append(pltpu.make_async_copy(x_hbm.at[:, part_of], x_ref.at[:, part_of], in_sem.at[3 + k]))
    for fetch in fetches:
        fetch.start()

    barrier = pltpu.get_barrier_semaphore()
    for peer in (
        [at_z(s) for s in range(1, NZ)] + [at_y(s) for s in range(1, NY)] + [at_t(s) for s in range(1, NT)]
    ):
        pl.semaphore_signal(barrier, inc=1, device_id=peer, device_id_type=pl.DeviceIdType.MESH)

    phase = start_ref[0] * lax.broadcasted_iota(jnp.int32, (8, NFFT), 1) % NFFT
    angle = 2.0 * jnp.pi / NFFT * phase.astype(jnp.float32)
    shift_cos = jnp.concatenate([jnp.cos(angle)] * 2, axis=0)
    shift_sin = jnp.concatenate([jnp.sin(angle)] * 2, axis=0)
    fetches[2].wait()
    for i in range(FQ):
        cos_i, sin_i = fixed[0, NT * i:NT * (i + 1)], fixed[1, NT * i:NT * (i + 1)]
        table_ref[32 * i:32 * i + 16] = (shift_cos * cos_i - shift_sin * sin_i).astype(jnp.bfloat16)
        table_ref[32 * i + 16:32 * i + 32] = (-(shift_sin * cos_i + shift_cos * sin_i)).astype(jnp.bfloat16)
    table_ref[ROWS:] = jnp.zeros((PAD - ROWS, NFFT), jnp.bfloat16)

    fetches[0].wait()
    ids = chan * CH + lax.broadcasted_iota(jnp.int32, (CH, DEAD), 0)
    struck = jnp.where(ids == jnp.broadcast_to(dead_ref[...][None, :], (CH, DEAD)), 1.0, 0.0)
    live_rows = jnp.broadcast_to(1.0 - jnp.max(struck, axis=1, keepdims=True), (CH, PAD))

    for k in range(4):
        fetches[3 + k].wait()
        blocks = [x_ref[:, (4 * k + b) * NFFT:(4 * k + b + 1) * NFFT] for b in range(4)]
        values = dot_nt(jnp.concatenate(blocks, axis=0), table_ref[...])
        for b in range(4):
            value = values[CH * b:CH * (b + 1)]
            sums[4 * k + b:4 * k + b + 1] = jnp.sum(value * live_rows, axis=0, keepdims=True)
    for q in range(3):
        lanes = slice(64 * q, 64 * q + 64)
        part[q] = jnp.concatenate([sums[0:8, lanes], sums[8:16, lanes]], axis=1)

    pl.semaphore_wait(barrier, (NZ - 1) + (NY - 1) + (NT - 1))

    pieces = (slice(0, 1), slice(1, 3))

    def sum_z(n):
        for s in range(1, NZ):
            start(
                "sum", part.at[pieces[n]], parts_in.at[s - 1, pieces[n]],
                ps_send.at[n, s - 1], ps_recv.at[n, s - 1], at_z(s),
            )

    def sum_y(n):
        total = part[pieces[n]]
        for s in range(1, NZ):
            arrived(parts_in.at[s - 1, pieces[n]], ps_recv.at[n, s - 1])
            total = total + parts_in[s - 1, pieces[n]]
        line[pieces[n]] = total
        for s in range(1, NY):
            start(
                "sum", line.at[pieces[n]], lines_in.at[s - 1, pieces[n]],
                ps_send.at[n, 6 + s], ps_recv.at[n, 6 + s], at_y(s),
            )

    def close_sum(n):
        total = line[pieces[n]]
        for s in range(1, NY):
            arrived(lines_in.at[s - 1, pieces[n]], ps_recv.at[n, 6 + s])
            total = total + lines_in[s - 1, pieces[n]]
        common[pieces[n]] = total / (NCHAN - DEAD)

    def transform(b, carry):
        samples = x_ref[:, pl.ds(pl.multiple_of(b * NFFT, NFFT), NFFT)]
        raw[pl.ds(b, ROWS, stride=NT), :] = dot_nt(table_ref[0:ROWS], samples)
        return carry

    sum_z(0)
    sum_z(1)
    live = live_rows[:, 0:CH].T[0:8]
    fetches[1].wait()
    source_ids = chan * CH + lax.broadcasted_iota(jnp.int32, (SRC, CH), 1)
    source_rows = lax.broadcasted_iota(jnp.int32, (SRC, CH), 0)
    wanted = jnp.zeros((SRC, CH), jnp.int32)
    for k in range(SRC):
        wanted = jnp.where(source_rows == k, source_ref[k], wanted)
    sel_ref[...] = jnp.where(wanted == source_ids, 1.0, 0.0).astype(jnp.bfloat16)
    lax.fori_loop(0, NT // 2, transform, 0)
    sum_y(0)
    sum_y(1)
    lax.fori_loop(NT // 2, NT, transform, 0)

    def give(group):
        first, last = GROUPS[group]
        for i in range(first, last):
            mode = common[i // 2]
            for p in range(2):
                for d in range(NT):
                    both = []
                    for half in range(2):
                        lane = 64 * half + 32 * (i % 2) + 16 * p + d
                        row = NT * (32 * i + 16 * p + d) + 8 * half
                        value = raw[row:row + 8]
                        both.append(live * (value - jnp.broadcast_to(mode[:, lane:lane + 1], (8, CH))))
                    send[i, d, p] = jnp.concatenate(both, axis=0).astype(jnp.bfloat16)
        for s in FAR_FIRST:
            remote(
                send.at[first:last, ts[s]], band.at[first:last, tm],
                re_send.at[group], re_recv.at[group], at_t(s),
            ).start()
        for i in range(first, last):
            band[i, tm] = send[i, tm]

    def whiten(i):
        real = band[i, :, 0].reshape(BLOCKS, CH).astype(jnp.float32)
        imag = band[i, :, 1].reshape(BLOCKS, CH).astype(jnp.float32)
        power = jnp.sum(real * real + imag * imag, axis=0, keepdims=True) / BLOCKS
        scale = lax.rsqrt(power + EPS)
        real, imag = real * scale, imag * scale
        mats[i, 0:BLOCKS, 0:CH] = real.astype(jnp.bfloat16)
        mats[i, BLOCKS:, 0:CH] = imag.astype(jnp.bfloat16)
        mats[i, 0:BLOCKS, CH:] = imag.astype(jnp.bfloat16)
        mats[i, BLOCKS:, CH:] = (-real).astype(jnp.bfloat16)
        rows = dot_nt(sel_ref[...], mats[i, :, 0:CH]).astype(jnp.bfloat16)
        for h in range(2):
            kind, u = UNITS[(i, h)]
            piece = rows[HALF * h:HALF * (h + 1)]
            if kind == 1:
                g1[u, z, 0] = piece
            else:
                g2[u, y, z] = piece

    def first_y(u, stage):
        if stage == 0:
            mine = g1.at[u, z, 0]
            start((Y1, u), mine, g1.at[u, z, 3], s1.at[u, 0], r1.at[u, 0], at_y(1))
            start((Y1, u), mine, g1.at[u, z, 1], s1.at[u, 1], r1.at[u, 1], at_y(-1))
        else:
            if u % 2 == 0:
                arrived(g1.at[u, z, 3], r1.at[u, 0])
                start((Y1, u), g1.at[u, z, 3], g1.at[u, z, 2], s1.at[u, 2], r1.at[u, 2], at_y(1))
                arrived(g1.at[u, z, 1], r1.at[u, 1])
            else:
                arrived(g1.at[u, z, 1], r1.at[u, 1])
                start((Y1, u), g1.at[u, z, 1], g1.at[u, z, 2], s1.at[u, 2], r1.at[u, 2], at_y(-1))
                arrived(g1.at[u, z, 3], r1.at[u, 0])

    def own_z(u, stage):
        left, right = zs[-stage % NZ], zs[stage]
        if stage == 4:
            arrived(g1.at[u, left, 0], r1.at[u, 17])
            return
        a, b = g1.at[u, left, 0], g1.at[u, right, 0]
        if stage > 0:
            arrived(a, r1.at[u, 9 + 2 * stage])
        if stage < 3 or u % 2 == 1:
            to = 17 if stage == 3 else 11 + 2 * stage
            start((OWN1, u), a, a, s1.at[u, to], r1.at[u, to], at_z(1))
        if stage > 0:
            arrived(b, r1.at[u, 10 + 2 * stage])
        if stage < 3 or u % 2 == 0:
            to = 17 if stage == 3 else 12 + 2 * stage
            start((OWN1, u), b, b, s1.at[u, to], r1.at[u, to], at_z(-1))

    def then_z(u, stage):
        low = 1 if u in EARLY else 0
        middle = 2 if low == 0 or u % 2 == 1 else 3
        left, right = zs[-stage % NZ], zs[stage]
        if stage == 4:
            arrived(g1.at[u, left, low:middle], r1.at[u, 9])
            arrived(g1.at[u, left, middle:4], r1.at[u, 10])
            if low:
                own_z(u, 4)
            lines(u, (4,))
            return
        if stage < 3:
            a, b = g1.at[u, left, low:4], g1.at[u, right, low:4]
        else:
            a, b = g1.at[u, left, low:middle], g1.at[u, right, middle:4]
        if stage == 0:
            arrived(g1.at[u, z, 2], r1.at[u, 2])
        else:
            arrived(g1.at[u, left, low:4], r1.at[u, 1 + 2 * stage])
        start((Z1, u, stage == 3), a, a, s1.at[u, 3 + 2 * stage], r1.at[u, 3 + 2 * stage], at_z(1))
        if stage > 0:
            arrived(g1.at[u, right, low:4], r1.at[u, 2 + 2 * stage])
        start((Z1, u, stage == 3), b, b, s1.at[u, 4 + 2 * stage], r1.at[u, 4 + 2 * stage], at_z(-1))
        if stage == 3:
            for steps in ((-3, -2, -1, 0), (1, 2, 3)):
                lines(u, steps)
            for key in ((Y1, u), (OWN1, u), (Z1, u, False)):
                settle(key)

    def lines(u, steps):
        i, h = PLACE[(1, u)]
        at = [zs[step % NZ] for step in steps]
        left = jnp.concatenate([g1[u, zz].reshape(NY * HALF, 2 * BLOCKS) for zz in at], axis=0)
        both = jnp.dot(left, mats[i], preferred_element_type=jnp.float32) * (1.0 / BLOCKS)
        both = both.astype(jnp.bfloat16).reshape(len(steps), NY, HALF, 2 * CH)
        for k, zz in enumerate(at):
            for up in range(NY):
                out_ref[0, i, ys[up], zz, h] = both[k, up, :, 0:CH]
                out_ref[1, i, ys[up], zz, h] = both[k, up, :, CH:]

    def first_z(u, stage):
        left, right = zs[-stage % NZ], zs[stage]
        a, b = g2.at[u, y, left], g2.at[u, y, right]
        if stage > 0:
            arrived(a, r2.at[u, 2 * stage - 2])
        if stage < 3 or u % 2 == 0:
            start((Z2, u), a, a, s2.at[u, 2 * stage], r2.at[u, 2 * stage], at_z(1))
        if stage > 0:
            arrived(b, r2.at[u, 2 * stage - 1])
        if stage < 3 or u % 2 == 1:
            start((Z2, u), b, b, s2.at[u, 2 * stage + 1], r2.at[u, 2 * stage + 1], at_z(-1))

    def then_y(u, stage):
        down, up, far = ys[3], ys[1], ys[2]
        if stage == 0:
            arrived(g2.at[u, y, zs[4]], r2.at[u, 6 + u % 2])
            start((Y2, u, 0), g2.at[u, y], g2.at[u, y], s2.at[u, 8], r2.at[u, 8], at_y(1))
            start((Y2, u, 0), g2.at[u, y], g2.at[u, y], s2.at[u, 9], r2.at[u, 9], at_y(-1))
        elif stage == 1:
            a, b = g2.at[u, down, 0:4], g2.at[u, up, 4:8]
            arrived(g2.at[u, down], r2.at[u, 8])
            start((Y2, u, 1), a, a, s2.at[u, 10], r2.at[u, 10], at_y(1))
            arrived(g2.at[u, up], r2.at[u, 9])
            start((Y2, u, 1), b, b, s2.at[u, 11], r2.at[u, 11], at_y(-1))
            columns(u, (-1, 0, 1))
            settle((Z2, u))
        else:
            arrived(g2.at[u, far, 0:4], r2.at[u, 10])
            arrived(g2.at[u, far, 4:8], r2.at[u, 11])
            columns(u, (2,))
            settle((Y2, u, 0))

    def columns(u, steps):
        i, h = PLACE[(2, u)]
        at = [ys[step % NY] for step in steps]
        left = jnp.concatenate([g2[u, yy].reshape(NZ * HALF, 2 * BLOCKS) for yy in at], axis=0)
        both = jnp.dot(left, mats[i], preferred_element_type=jnp.float32) * (1.0 / BLOCKS)
        both = both.astype(jnp.bfloat16).reshape(len(steps), NZ, HALF, 2 * CH)
        for k, yy in enumerate(at):
            out_ref[0, i, yy, :, h] = both[k, :, :, 0:CH]
            out_ref[1, i, yy, :, h] = both[k, :, :, CH:]

    def take(group):
        first, last = GROUPS[group]
        arrived(band.at[first:last, 0:NT - 1], re_recv.at[group])
        for i in range(first, last):
            whiten(i)

    def free(group):
        first, last = GROUPS[group]
        arrived(send.at[first:last, 0:NT - 1], re_send.at[group])

    steps = (take, first_y, then_z, own_z, first_z, then_y)
    close_sum(0)
    give(0)
    close_sum(1)
    give(1)
    for at, (step, unit, stage) in enumerate(ORDER):
        if at == LATE:
            give(2)
        if at == LATE + 44:
            settle("sum")
            for group in range(len(GROUPS)):
                free(group)
        if step == TAKE:
            take(unit)
        else:
            steps[step](unit, stage)
    for key in list(sent):
        settle(key)


def body(strain_record, dead_channels, source_channels, band_start):
    vmem = pl.BlockSpec(memory_space=pltpu.VMEM)
    hbm = pl.BlockSpec(memory_space=pltpu.HBM)
    dma = pltpu.SemaphoreType.DMA
    out = pl.pallas_call(
        kernel,
        out_shape=jax.ShapeDtypeStruct((2, FQ, NY, NZ, 2, HALF, CH), jnp.bfloat16),
        in_specs=[hbm] * 4 + [pl.BlockSpec(memory_space=pltpu.SMEM)],
        out_specs=vmem,
        scratch_shapes=[
            pltpu.VMEM((CH, NT * NFFT), jnp.bfloat16),
            pltpu.VMEM((2, FQ * NT, NFFT), jnp.float32),
            pltpu.VMEM((DEAD,), jnp.int32),
            pltpu.SMEM((SRC,), jnp.int32),
            pltpu.VMEM((PAD, NFFT), jnp.bfloat16),
            pltpu.VMEM((SRC, CH), jnp.bfloat16),
            pltpu.VMEM((NT * ROWS, CH), jnp.float32),
            pltpu.VMEM((NT, PAD), jnp.float32),
            pltpu.VMEM((3, 8, CH), jnp.float32),
            pltpu.VMEM((NZ - 1, 3, 8, CH), jnp.float32),
            pltpu.VMEM((3, 8, CH), jnp.float32),
            pltpu.VMEM((NY - 1, 3, 8, CH), jnp.float32),
            pltpu.VMEM((3, 8, CH), jnp.float32),
            pltpu.VMEM((FQ, NT, 2, NT, CH), jnp.bfloat16),
            pltpu.VMEM((FQ, NT, 2, NT, CH), jnp.bfloat16),
            pltpu.VMEM((FQ, 2 * BLOCKS, 2 * CH), jnp.bfloat16),
            pltpu.VMEM((NP1, NZ, NY, HALF, 2 * BLOCKS), jnp.bfloat16),
            pltpu.VMEM((NP2, NY, NZ, HALF, 2 * BLOCKS), jnp.bfloat16),
            dma((7,)), dma((2, 10)), dma((2, 10)), dma((3,)), dma((3,)),
            dma((NP1, 18)), dma((NP1, 18)), dma((NP2, 12)), dma((NP2, 12)),
        ],
        compiler_params=pltpu.CompilerParams(
            collective_id=0, has_side_effects=True, vmem_limit_bytes=48 * 1024 * 1024
        ),
    )(*[
        pltpu.with_memory_space_constraint(array, pltpu.HBM)
        for array in (strain_record, jnp.asarray(fixed_tables()), dead_channels, source_channels)
    ], band_start)
    return out.reshape(2, FQ, NY * NZ * SRC, CH)


def solution(mesh):
    in_specs = (P("chan", "tm"), P(), P("chan"), P())
    out_specs = P(None, "tm", None, "chan")
    return jax.shard_map(body, mesh=mesh, in_specs=in_specs, out_specs=out_specs, check_vma=False)
```
